512 devices in a mesh: fsdp: 32 (over z, x_hi), seq: 16 (over y, x_lo, core).
Axes of the slice: x: 4 (x_hi: 2, x_lo: 2; x = x_hi * 2 + x_lo), y: 4, z: 16, core: 2. Of those that a mesh axis runs over, the one named last changes fastest.
Arguments:
- queries: bfloat16 [32, 16, 128, 2560], P('fsdp', 'seq'), may hold values from -60 to 60
- keys: bfloat16 [32, 16, 128, 2560], P('fsdp', 'seq'), may hold values from -60 to 60
- values: bfloat16 [32, 16, 128, 2560], P('fsdp', 'seq'), may hold values from -6 to 6
- grad_out: bfloat16 [32, 16, 128, 2560], P('fsdp', 'seq'), may hold values from -6 to 6
- q_gain: float32 [2560], P('fsdp'), may hold values from 0.5 to 1.5
- k_gain: float32 [2560], P('fsdp'), may hold values from 0.5 to 1.5
- lengths: int32 [32], P('fsdp'), may hold values from 1 to 16, as said below
- windows: int32 [20, 3], replicated, may hold values from 0 to 1, as said below
Outputs:
- d_queries: bfloat16 [32, 16, 128, 2560], P('fsdp', 'seq')
- d_keys: bfloat16 [32, 16, 128, 2560], P('fsdp', 'seq')
- d_values: bfloat16 [32, 16, 128, 2560], P('fsdp', 'seq')
- d_q_gain: float32 [2560], P('fsdp')
- d_k_gain: float32 [2560], P('fsdp')
The draws below stay inside these ranges and needn't reach their ends.
Inputs may be any that keep to these rules, and one draw needn't show every extreme that they name: `lengths`: some clip has all 16 frames. `windows`: frame half-widths reach 1 in some head; tile half-widths are 0 or 1.
All inputs are finite; a program needn't handle non-finite values.
Results may differ from the reference program's by a relative error of at most 0.012.
The reference program's roundings to bfloat16 on the way (of `query_normed`, `weights` and `dscores`) count: a program that leaves them out, or rounds other values in their place, can miss the bound.
Values may be sent and summed in bfloat16 or wider, within the bound.
A program may use at most 128 MiB of HBM per device.

```python
import jax
import jax.numpy as jnp
from jax import lax

HEADS = 20
HD = 128
FD = 1
PW = 8
TILE_H = 4
TILE_W = 4
HC = 2560
PIX = 128
FRAMES = 16
CLIPS = 32


def draw_queries(key, part):
    key = jax.random.fold_in(key, 3)
    independent = jnp.clip(jax.random.normal(key, (CLIPS, FRAMES, PIX, HC), jnp.float32), -6.0, 6.0)
    return independent.astype(jnp.bfloat16)


def draw_keys(key, part):
    key = jax.random.fold_in(key, 5)
    independent = jnp.clip(jax.random.normal(key, (CLIPS, FRAMES, PIX, HC), jnp.float32), -6.0, 6.0)
    return independent.astype(jnp.bfloat16)


def draw_lengths(key, part):
    key = jax.random.fold_in(key, 7)
    counts = jax.random.randint(key, (CLIPS,), 1, FRAMES + 1, dtype=jnp.int32)
    longest = jax.random.randint(jax.random.fold_in(key, 1), (), 0, CLIPS, dtype=jnp.int32)
    return counts.at[longest].set(FRAMES)


def draw_windows(key, part):
    key = jax.random.fold_in(key, 9)
    temporal = jax.random.randint(key, (HEADS, 1), 0, FD + 1, dtype=jnp.int32)
    spatial = jax.random.randint(jax.random.fold_in(key, 1), (HEADS, 2), 0, 2, dtype=jnp.int32)
    widest = jax.random.randint(jax.random.fold_in(key, 2), (), 0, HEADS, dtype=jnp.int32)
    temporal = temporal.at[widest, 0].set(FD)
    return jnp.concatenate([temporal, spatial], 1)


def steps_of(key, dims, split, low, top_value):
    gain, own = 1.0, jax.random.fold_in(key, 6)
    for axis_at, parts in split:
        steps = jnp.exp(jax.random.uniform(jax.random.fold_in(own, axis_at), (parts,), jnp.float32, low / len(split), top_value / len(split)))
        gain = gain * jnp.repeat(steps, dims[axis_at] // parts).reshape([-1 if axis == axis_at else 1 for axis in range(len(dims))])
    return gain


def centred(rng, extent, deviation, bound, split=(), kind=jnp.bfloat16):
    drawn = deviation * jax.random.normal(rng, extent, jnp.float32)
    if split:
        drawn = drawn * steps_of(rng, extent, split, -0.22, 0.18)
    return jnp.clip(drawn, -bound, bound).astype(kind)


def setup_inputs(seed: int = 0) -> dict:
    streams_of = jax.random.split(jax.random.key(seed), 9)
    return {
        "queries": draw_queries(jax.random.fold_in(streams_of[8], 71), 0),
        "keys": draw_keys(jax.random.fold_in(streams_of[8], 71), 0),
        "values": centred(streams_of[2], (CLIPS, FRAMES, PIX, HC), 1.0, 6.0, ((0, 32), (1, 16))),
        "grad_out": centred(streams_of[3], (CLIPS, FRAMES, PIX, HC), 1.0, 6.0, ((0, 32), (1, 16))),
        "q_gain": jnp.clip(1.0 + 0.1 * jax.random.normal(streams_of[4], (HC,), jnp.float32), 0.5, 1.5),
        "k_gain": jnp.clip(1.0 + 0.1 * jax.random.normal(streams_of[5], (HC,), jnp.float32), 0.5, 1.5),
        "lengths": draw_lengths(jax.random.fold_in(streams_of[8], 71), 0),
        "windows": draw_windows(jax.random.fold_in(streams_of[8], 71), 0),
    }


def positions(first_frame, frame_count, pixels):
    row_index = jnp.arange(frame_count * pixels, dtype=jnp.int32)
    frame_of = first_frame + row_index // pixels
    pixel_of = row_index % pixels
    return (frame_of, pixel_of // PW // TILE_H, pixel_of % PW // TILE_W)

def within_reach(left, right, limit):
    return jnp.abs(left[:, None] - right[None, :])[None] <= limit[:, None, None]

def window_mask(query_pos, key_pos, windows, length):
    inside = within_reach(query_pos[0], key_pos[0], windows[:, 0])
    inside = inside & within_reach(query_pos[1], key_pos[1], windows[:, 1])
    inside = inside & within_reach(query_pos[2], key_pos[2], windows[:, 2])
    key_valid = (key_pos[0] >= 0) & (key_pos[0] < length)
    query_valid = (query_pos[0] >= 0) & (query_pos[0] < length)
    return inside & key_valid[None, None, :] & query_valid[None, :, None]

def contract(form, left, right):
    return jnp.einsum(form, left.astype(jnp.float32), right.astype(jnp.float32))

def query_side(query_normed, key_normed, value_rows, upstream, allowed, factor):
    scores = contract('qhd,khd->hqk', query_normed, key_normed) * factor
    summit = lax.optimization_barrier(jnp.max(jnp.where(allowed, scores, -1e+30), -1))
    alive = jnp.any(allowed, -1)
    summit = jnp.where(alive, summit, 0.0)
    totals = lax.optimization_barrier(jnp.sum(jnp.where(allowed, jnp.exp(scores - summit[..., None]), 0.0), -1))
    totals = totals + jnp.where(alive, 0.0, 1.0)
    logsum = summit + jnp.log(totals)
    probs = jnp.where(allowed, jnp.exp(scores - logsum[..., None]), 0.0)
    weights = probs.astype(jnp.bfloat16)
    attended = contract('hqk,khd->qhd', weights, value_rows)
    deltas = lax.optimization_barrier(jnp.sum(upstream.astype(jnp.float32) * attended, -1))
    dprobs = contract('qhd,khd->hqk', upstream, value_rows)
    dscores = (probs * (dprobs - deltas.T[:, :, None])).astype(jnp.bfloat16)
    query_grad = contract('hqk,khd->qhd', dscores, key_normed) * factor
    return (logsum.T, deltas, query_grad)

def key_side(query_normed, upstream, logsum, deltas, key_normed, value_rows, allowed, factor):
    scores = contract('qhd,khd->hqk', query_normed, key_normed) * factor
    probs = jnp.where(allowed, jnp.exp(scores - logsum.T[:, :, None]), 0.0)
    weights = probs.astype(jnp.bfloat16)
    value_grad = contract('hqk,qhd->khd', weights, upstream)
    dprobs = contract('qhd,khd->hqk', upstream, value_rows)
    dscores = (probs * (dprobs - deltas.T[:, :, None])).astype(jnp.bfloat16)
    key_grad = contract('hqk,qhd->khd', dscores, query_normed) * factor
    return (key_grad, value_grad)

def normed(row_data, gain_vec):
    widened = row_data.astype(jnp.float32)
    inverse = lax.rsqrt(lax.optimization_barrier(jnp.mean(widened * widened, -1, keepdims=True)) + 1e-06)
    return ((widened * inverse * gain_vec).astype(jnp.bfloat16), widened, inverse)

def norm_back(upstream, widened, inverse, gain_vec):
    scaled = upstream * gain_vec
    inner = lax.optimization_barrier(jnp.mean(scaled * widened, -1, keepdims=True))
    grad_rows = inverse * (scaled - widened * inverse * inverse * inner)
    return (grad_rows.astype(jnp.bfloat16), lax.optimization_barrier(jnp.sum(upstream * widened * inverse, 0)))

def widen_rows(array_in, margin):
    padding = jnp.zeros((margin,) + array_in.shape[1:], array_in.dtype)
    return jnp.concatenate([padding, array_in, padding], 0)

def one_clip(q_gain, k_gain, windows, clip_data):
    query_in, key_in, value_in, upstream_in, length = clip_data
    row_count = FRAMES * PIX
    slab_rows = FD * PIX
    factor = HD ** (-0.5)
    query_normed, query_wide, query_inv = normed(query_in.reshape(row_count, HC), q_gain)
    key_normed, key_wide, key_inv = normed(key_in.reshape(row_count, HC), k_gain)
    query_heads = query_normed.reshape(row_count, HEADS, HD)
    key_heads = key_normed.reshape(row_count, HEADS, HD)
    value_heads = value_in.reshape(row_count, HEADS, HD)
    upstream_heads = upstream_in.reshape(row_count, HEADS, HD)
    key_padded = widen_rows(key_heads, slab_rows)
    value_padded = widen_rows(value_heads, slab_rows)

    def front(slab_index):
        start = (slab_index * slab_rows).astype(jnp.int32)
        own_query = lax.dynamic_slice_in_dim(query_heads, start, slab_rows, 0)
        own_upstream = lax.dynamic_slice_in_dim(upstream_heads, start, slab_rows, 0)
        near_keys = lax.dynamic_slice_in_dim(key_padded, start, 3 * slab_rows, 0)
        near_values = lax.dynamic_slice_in_dim(value_padded, start, 3 * slab_rows, 0)
        query_pos = positions(slab_index * FD, FD, PIX)
        key_pos = positions(slab_index * FD - FD, 3 * FD, PIX)
        allowed = window_mask(query_pos, key_pos, windows, length)
        return query_side(own_query, near_keys, near_values, own_upstream, allowed, factor)
    logsum, deltas, query_grad = lax.map(front, jnp.arange(FRAMES // FD, dtype=jnp.int32))
    logsum = widen_rows(logsum.reshape(row_count, HEADS), slab_rows)
    deltas = widen_rows(deltas.reshape(row_count, HEADS), slab_rows)
    query_padded = widen_rows(query_heads, slab_rows)
    upstream_padded = widen_rows(upstream_heads, slab_rows)

    def back(slab_index):
        start = (slab_index * slab_rows).astype(jnp.int32)
        own_keys = lax.dynamic_slice_in_dim(key_heads, start, slab_rows, 0)
        own_values = lax.dynamic_slice_in_dim(value_heads, start, slab_rows, 0)
        near_query = lax.dynamic_slice_in_dim(query_padded, start, 3 * slab_rows, 0)
        near_upstream = lax.dynamic_slice_in_dim(upstream_padded, start, 3 * slab_rows, 0)
        near_logsum = lax.dynamic_slice_in_dim(logsum, start, 3 * slab_rows, 0)
        near_deltas = lax.dynamic_slice_in_dim(deltas, start, 3 * slab_rows, 0)
        query_pos = positions(slab_index * FD - FD, 3 * FD, PIX)
        key_pos = positions(slab_index * FD, FD, PIX)
        allowed = window_mask(query_pos, key_pos, windows, length)
        return key_side(near_query, near_upstream, near_logsum, near_deltas, own_keys, own_values, allowed, factor)
    key_grad, value_grad = lax.map(back, jnp.arange(FRAMES // FD, dtype=jnp.int32))
    query_out, query_gain_grad = norm_back(query_grad.reshape(row_count, HC), query_wide, query_inv, q_gain)
    key_out, key_gain_grad = norm_back(key_grad.reshape(row_count, HC), key_wide, key_inv, k_gain)
    value_out = value_grad.reshape(row_count, HC).astype(jnp.bfloat16)
    array_shape = (FRAMES, PIX, HC)
    return (query_out.reshape(array_shape), key_out.reshape(array_shape), value_out.reshape(array_shape), query_gain_grad, key_gain_grad)

def reference(queries, keys, values, grad_out, q_gain, k_gain, lengths, windows):

    def run_clip(clip_data):
        return one_clip(q_gain, k_gain, windows, clip_data)
    d_queries, d_keys, d_values, query_gains, key_gains = lax.map(run_clip, (queries, keys, values, grad_out, lengths))
    return (d_queries, d_keys, d_values, lax.optimization_barrier(jnp.sum(query_gains, 0)), lax.optimization_barrier(jnp.sum(key_gains, 0)))
```

```python
import jax
import jax.numpy as jnp
from jax import lax
from jax.experimental import pallas as pl
from jax.experimental.pallas import tpu as pltpu
from jax.sharding import PartitionSpec as P

PW = 8
TILE_H = 4
TILE_W = 4
MESH = pl.DeviceIdType.MESH
LANES = 128


def gather_gains_kernel(count, q_ref, k_ref, out_ref, mine, inbox, send_sem, recv_sem):
    me = lax.axis_index("fsdp")
    width = q_ref.shape[1]
    barrier = pltpu.get_barrier_semaphore()

    def greet(step, carry):
        peer = lax.rem(me + step, count)
        pl.semaphore_signal(barrier, inc=1, device_id={"fsdp": peer}, device_id_type=MESH)
        return carry

    lax.fori_loop(1, count, greet, 0)
    mine[...] = jnp.zeros_like(mine)
    mine[0:1, 0:width] = q_ref[...]
    mine[0:1, LANES : LANES + width] = k_ref[...]
    inbox[pl.ds(me, 1)] = mine[...][None]
    pl.semaphore_wait(barrier, count - 1)

    def copy(step):
        peer = lax.rem(me + step, count)
        return pltpu.make_async_remote_copy(
            src_ref=mine,
            dst_ref=inbox.at[me],
            send_sem=send_sem.at[step],
            recv_sem=recv_sem.at[step],
            device_id={"fsdp": peer},
            device_id_type=MESH,
        )

    def start(step, carry):
        copy(step).start()
        return carry

    def finish(step, carry):
        copy(step).wait()
        return carry

    lax.fori_loop(1, count, start, 0)
    lax.fori_loop(1, count, finish, 0)
    lane = lax.broadcasted_iota(jnp.int32, (1, LANES), 1)
    for row in range(2):
        tiles = [jnp.zeros((1, LANES), jnp.float32) for _ in range(out_ref.shape[1] // LANES + 1)]
        for owner in range(count):
            tile, offset = divmod(owner * width, LANES)
            part = inbox[owner, :, row * LANES : (row + 1) * LANES]
            if offset:
                part = pltpu.roll(part, offset, 1)
            if offset + width > LANES:
                tiles[tile + 1] = tiles[tile + 1] + jnp.where(lane < offset, part, 0.0)
                part = jnp.where(lane >= offset, part, 0.0)
            tiles[tile] = tiles[tile] + part
        for at in range(out_ref.shape[1] // LANES):
            out_ref[row : row + 1, at * LANES : (at + 1) * LANES] = tiles[at]


def gather_gains(q_gain, k_gain):
    count = lax.axis_size("fsdp")
    width = q_gain.shape[0]
    return pl.pallas_call(
        lambda *refs: gather_gains_kernel(count, *refs),
        out_shape=jax.ShapeDtypeStruct((2, count * width), jnp.float32),
        in_specs=[pl.BlockSpec(memory_space=pltpu.VMEM)] * 2,
        out_specs=pl.BlockSpec(memory_space=pltpu.VMEM),
        scratch_shapes=[
            pltpu.VMEM((1, 2 * LANES), jnp.float32),
            pltpu.VMEM((count, 1, 2 * LANES), jnp.float32),
            pltpu.SemaphoreType.DMA((count,)),
            pltpu.SemaphoreType.DMA((count,)),
        ],
        compiler_params=pltpu.CompilerParams(collective_id=0, has_side_effects=True),
        name="gather_gains",
    )(q_gain[None], k_gain[None])


def reduce_gains_kernel(
    count, group, gains_ref, q_ref, k_ref, outbox, inbox, mine, inbox_seq, send_sem, recv_sem, send_seq, recv_seq
):
    me = lax.axis_index("fsdp")
    rank = lax.axis_index("seq")
    width = q_ref.shape[1]
    barrier = pltpu.get_barrier_semaphore()

    def greet(step, carry):
        peer = lax.rem(me + step, count)
        pl.semaphore_signal(barrier, inc=1, device_id={"fsdp": peer}, device_id_type=MESH)
        return carry

    def greet_seq(step, carry):
        peer = lax.rem(rank + step, group)
        pl.semaphore_signal(barrier, inc=1, device_id={"seq": peer}, device_id_type=MESH)
        return carry

    lax.fori_loop(1, count, greet, 0)
    lax.fori_loop(1, group, greet_seq, 0)
    lane = lax.broadcasted_iota(jnp.int32, (1, LANES), 1)
    for owner in range(count):
        tile, offset = divmod(owner * width, LANES)
        for row in range(2):
            part = gains_ref[row : row + 1, tile * LANES : (tile + 1) * LANES]
            if offset:
                part = pltpu.roll(part, LANES - offset, 1)
            if offset + width > LANES:
                after = gains_ref[row : row + 1, (tile + 1) * LANES : (tile + 2) * LANES]
                after = pltpu.roll(after, LANES - offset, 1)
                part = jnp.where(lane < LANES - offset, part, after)
            outbox[owner, :, row * LANES : (row + 1) * LANES] = part
    inbox[pl.ds(me, 1)] = outbox[pl.ds(me, 1)]
    pl.semaphore_wait(barrier, count + group - 2)

    def copy(step):
        peer = lax.rem(me + step, count)
        return pltpu.make_async_remote_copy(
            src_ref=outbox.at[peer],
            dst_ref=inbox.at[me],
            send_sem=send_sem.at[step],
            recv_sem=recv_sem.at[step],
            device_id={"fsdp": peer},
            device_id_type=MESH,
        )

    def copy_seq(step):
        peer = lax.rem(rank + step, group)
        return pltpu.make_async_remote_copy(
            src_ref=mine,
            dst_ref=inbox_seq.at[rank],
            send_sem=send_seq.at[step],
            recv_sem=recv_seq.at[step],
            device_id={"seq": peer},
            device_id_type=MESH,
        )

    def start(step, carry):
        copy(step).start()
        return carry

    def finish(step, carry):
        copy(step).wait()
        return carry

    def start_seq(step, carry):
        copy_seq(step).start()
        return carry

    def finish_seq(step, carry):
        copy_seq(step).wait()
        return carry

    lax.fori_loop(1, count, start, 0)
    lax.fori_loop(1, count, finish, 0)
    mine[...] = jnp.sum(inbox[...], axis=0)
    lax.fori_loop(1, group, start_seq, 0)
    inbox_seq[pl.ds(rank, 1)] = mine[...][None]
    lax.fori_loop(1, group, finish_seq, 0)
    total = jnp.sum(inbox_seq[...], axis=0)
    q_ref[...] = total[:, 0:width]
    k_ref[...] = total[:, LANES : LANES + width]


def reduce_gains(gains):
    count, group = lax.axis_size("fsdp"), lax.axis_size("seq")
    width = gains.shape[1] // count
    q_part, k_part = pl.pallas_call(
        lambda *refs: reduce_gains_kernel(count, group, *refs),
        out_shape=[jax.ShapeDtypeStruct((1, width), jnp.float32)] * 2,
        in_specs=[pl.BlockSpec(memory_space=pltpu.VMEM)],
        out_specs=[pl.BlockSpec(memory_space=pltpu.VMEM)] * 2,
        scratch_shapes=[
            pltpu.VMEM((count, 1, 2 * LANES), jnp.float32),
            pltpu.VMEM((count, 1, 2 * LANES), jnp.float32),
            pltpu.VMEM((1, 2 * LANES), jnp.float32),
            pltpu.VMEM((group, 1, 2 * LANES), jnp.float32),
            pltpu.SemaphoreType.DMA((count,)),
            pltpu.SemaphoreType.DMA((count,)),
            pltpu.SemaphoreType.DMA((group,)),
            pltpu.SemaphoreType.DMA((group,)),
        ],
        compiler_params=pltpu.CompilerParams(collective_id=1, has_side_effects=True),
        name="reduce_gains",
    )(gains)
    return q_part[0], k_part[0]


def padded(block, sides, width):
    for axis, dim in sides:
        count = lax.axis_size(axis)
        forward = [(i, i + 1) for i in range(count - 1)]
        backward = [(target, source) for source, target in forward]
        low = lax.ppermute(
            lax.slice_in_dim(block, block.shape[dim] - width, None, axis=dim), axis, forward
        )
        high = lax.ppermute(lax.slice_in_dim(block, 0, width, axis=dim), axis, backward)
        block = jnp.concatenate([low, block, high], axis=dim)
    return block


def shifted(value, axis, steps):
    count = lax.axis_size(axis)
    first, last = (max(0, -steps), min(count, count - steps))
    return lax.ppermute(value, axis, [(source, source + steps) for source in range(first, last)])


def positions(first_frame, frame_count, pixels):
    row_index = jnp.arange(frame_count * pixels, dtype=jnp.int32)
    frame_of = first_frame + row_index // pixels
    pixel_of = row_index % pixels
    return (frame_of, pixel_of // PW // TILE_H, pixel_of % PW // TILE_W)


def within_reach(left, right, limit):
    return jnp.abs(left[:, None] - right[None, :])[None] <= limit[:, None, None]


def window_mask(query_pos, key_pos, windows, length):
    inside = within_reach(query_pos[0], key_pos[0], windows[:, 0])
    inside = inside & within_reach(query_pos[1], key_pos[1], windows[:, 1])
    inside = inside & within_reach(query_pos[2], key_pos[2], windows[:, 2])
    key_valid = (key_pos[0] >= 0) & (key_pos[0] < length)
    query_valid = (query_pos[0] >= 0) & (query_pos[0] < length)
    return inside & key_valid[None, None, :] & query_valid[None, :, None]


def contract(form, left, right):
    return jnp.einsum(form, left, right, preferred_element_type=jnp.float32)


def query_side(query_normed, key_normed, value_rows, upstream, allowed, factor):
    scores = contract("qhd,khd->hqk", query_normed, key_normed) * factor
    summit = jnp.max(jnp.where(allowed, scores, -1e30), -1)
    alive = jnp.any(allowed, -1)
    summit = jnp.where(alive, summit, 0.0)
    totals = jnp.sum(jnp.where(allowed, jnp.exp(scores - summit[..., None]), 0.0), -1)
    totals = totals + jnp.where(alive, 0.0, 1.0)
    logsum = summit + jnp.log(totals)
    probs = jnp.where(allowed, jnp.exp(scores - logsum[..., None]), 0.0)
    weights = probs.astype(jnp.bfloat16)
    attended = contract("hqk,khd->qhd", weights, value_rows)
    deltas = jnp.sum(upstream.astype(jnp.float32) * attended, -1)
    dprobs = contract("qhd,khd->hqk", upstream, value_rows)
    dscores = (probs * (dprobs - deltas.T[:, :, None])).astype(jnp.bfloat16)
    query_grad = contract("hqk,khd->qhd", dscores, key_normed) * factor
    return (logsum.T, deltas, query_grad, weights, dscores)


def normed(row_data, gain_vec):
    widened = row_data.astype(jnp.float32)
    inverse = lax.rsqrt(jnp.mean(widened * widened, -1, keepdims=True) + 1e-06)
    return ((widened * inverse * gain_vec).astype(jnp.bfloat16), widened, inverse)


def norm_back(upstream, widened, inverse, gain_vec):
    scaled = upstream * gain_vec
    inner = jnp.mean(scaled * widened, -1, keepdims=True)
    grad_rows = inverse * (scaled - widened * inverse * inverse * inner)
    return (grad_rows.astype(jnp.bfloat16), jnp.sum(upstream * widened * inverse, 0))


def local(queries, keys, values, grad_out, q_gain, k_gain, lengths, windows):
    frame_count, pixels, columns = (queries.shape[1], queries.shape[2], queries.shape[3])
    head_count = windows.shape[0]
    head_size = columns // head_count
    row_count = frame_count * pixels
    factor = head_size ** (-0.5)
    gains_full = gather_gains(q_gain, k_gain)
    query_gain_full, key_gain_full = gains_full[0], gains_full[1]
    query_normed, query_wide, query_inv = normed(
        queries.reshape(row_count, columns), query_gain_full
    )
    key_normed, key_wide, key_inv = normed(keys.reshape(row_count, columns), key_gain_full)
    value_rows = values.reshape(row_count, columns)
    upstream = grad_out.reshape(row_count, columns)
    length = lengths[0]
    first_frame = lax.axis_index("seq") * frame_count
    heads_view = (row_count, head_count, head_size)
    wide_view = (3 * row_count, head_count, head_size)
    stacked_keys = jnp.stack([key_normed, value_rows]).reshape(2, 1, frame_count, pixels, columns)
    key_window = padded(stacked_keys, (("seq", 2),), frame_count)
    near_keys = key_window[0].reshape(wide_view)
    near_values = key_window[1].reshape(wide_view)
    own_pos = positions(first_frame, frame_count, pixels)
    near_pos = positions(first_frame - frame_count, 3 * frame_count, pixels)
    allowed = window_mask(own_pos, near_pos, windows, length)
    query_heads = query_normed.reshape(heads_view)
    upstream_heads = upstream.reshape(heads_view)
    logsum, deltas, query_grad, weights, dscores = query_side(
        query_heads, near_keys, near_values, upstream_heads, allowed, factor
    )
    value_terms = contract("hqk,qhd->khd", weights, upstream_heads)
    key_terms = contract("hqk,qhd->khd", dscores, query_heads) * factor
    partials = jnp.stack([key_terms, value_terms]).reshape(2, 3, row_count, columns)
    from_above = shifted(partials[:, 0].astype(jnp.bfloat16), "seq", -1)
    from_below = shifted(partials[:, 2].astype(jnp.bfloat16), "seq", 1)
    combined = partials[:, 1] + from_above + from_below
    key_grad = combined[0]
    value_grad = combined[1]
    query_out, query_gain_grad = norm_back(
        query_grad.reshape(row_count, columns), query_wide, query_inv, query_gain_full
    )
    key_out, key_gain_grad = norm_back(key_grad, key_wide, key_inv, key_gain_full)
    value_out = value_grad.astype(jnp.bfloat16)
    shares = reduce_gains(jnp.stack([query_gain_grad, key_gain_grad]))
    out_shape = queries.shape
    return (
        query_out.reshape(out_shape),
        key_out.reshape(out_shape),
        value_out.reshape(out_shape),
        shares[0],
        shares[1],
    )


def solution(mesh):
    in_specs = (
        P("fsdp", "seq", None, None),
        P("fsdp", "seq", None, None),
        P("fsdp", "seq", None, None),
        P("fsdp", "seq", None, None),
        P("fsdp"),
        P("fsdp"),
        P("fsdp"),
        P(),
    )
    out_specs = (
        P("fsdp", "seq", None, None),
        P("fsdp", "seq", None, None),
        P("fsdp", "seq", None, None),
        P("fsdp"),
        P("fsdp"),
    )
    return jax.shard_map(local, mesh=mesh, in_specs=in_specs, out_specs=out_specs, check_vma=False)
```

```python
import functools

import jax
import jax.numpy as jnp
from jax import lax
from jax.experimental import pallas as pl
from jax.experimental.pallas import tpu as pltpu
from jax.sharding import PartitionSpec as P

PW = 8
TILE_H = 4
TILE_W = 4
LANES = 128
EPS = 1e-06
BLOCKED = -1e30
FLOOR = -1e29
MESH = pl.DeviceIdType.MESH
KEYS, VALUES, QUERIES, UPSTREAM = range(4)


def dot(left, right, left_dim, right_dim):
    return lax.dot_general(
        left, right, (((left_dim,), (right_dim,)), ((), ())), preferred_element_type=jnp.float32
    )


def attention_kernel(
    far,
    count,
    group,
    limits,
    queries,
    keys,
    values,
    upstream,
    q_gain,
    k_gain,
    d_queries,
    d_keys,
    d_values,
    d_q_gain,
    d_k_gain,
    key_raw,
    query_raw,
    key_own,
    query_own,
    value_own,
    upstream_own,
    key_in,
    value_in,
    query_in,
    upstream_in,
    stat_out,
    stat_in,
    inverse_out,
    inverse_in,
    inverse_own,
    inverse_near,
    gains,
    gain_rows,
    query_grad,
    key_grad,
    value_grad,
    gain_mine,
    gain_inbox,
    sum_outbox,
    sum_inbox,
    sum_mine,
    sum_inbox_seq,
    send_sem,
    recv_sem,
    stat_send,
    stat_recv,
    inverse_send,
    inverse_recv,
    gain_send,
    gain_recv,
    sum_send,
    sum_recv,
    seq_send,
    seq_recv,
):
    me = lax.axis_index("fsdp")
    rank = lax.axis_index("seq")
    heads = limits.shape[0]
    rows, columns = queries.shape
    size = columns // heads
    width = q_gain.shape[1]
    factor = size ** (-0.5)
    far_pairs, pairs = far // 2, heads // 2
    below, above = lax.rem(rank + group - 1, group), lax.rem(rank + 1, group)
    barrier = pltpu.get_barrier_semaphore()

    def repeat(first, last, body):
        lax.fori_loop(first, last, lambda step, carry: (body(step), carry)[1], 0)

    def of_head(ref, head):
        return ref[:, pl.ds(pl.multiple_of(head * size, size), size)]

    outgoing = (key_raw, value_own, query_raw, upstream_own)
    incoming = (key_in, value_in, query_in, upstream_in)

    def link(which, side, pair):
        part = pl.ds(2 * pair, 2)
        return pltpu.make_async_remote_copy(
            src_ref=outgoing[which].at[part],
            dst_ref=incoming[which].at[1 - side, part],
            send_sem=send_sem.at[which, side, pair],
            recv_sem=recv_sem.at[which, 1 - side, pair],
            device_id={"seq": above if side else below},
            device_id_type=MESH,
        )

    def stat_link(side, pair):
        part = pl.ds(2 * pair, 2)
        return pltpu.make_async_remote_copy(
            src_ref=stat_out.at[part],
            dst_ref=stat_in.at[1 - side, part],
            send_sem=stat_send.at[side, pair],
            recv_sem=stat_recv.at[1 - side, pair],
            device_id={"seq": above if side else below},
            device_id_type=MESH,
        )

    def inverse_link(side):
        return pltpu.make_async_remote_copy(
            src_ref=inverse_out,
            dst_ref=inverse_in.at[1 - side],
            send_sem=inverse_send.at[side],
            recv_sem=inverse_recv.at[1 - side],
            device_id={"seq": above if side else below},
            device_id_type=MESH,
        )

    def gain_link(step):
        return pltpu.make_async_remote_copy(
            src_ref=gain_mine,
            dst_ref=gain_inbox.at[me],
            send_sem=gain_send.at[step],
            recv_sem=gain_recv.at[step],
            device_id={"fsdp": lax.rem(me + step, count)},
            device_id_type=MESH,
        )

    def sum_link(step):
        peer = lax.rem(me + step, count)
        return pltpu.make_async_remote_copy(
            src_ref=sum_outbox.at[peer],
            dst_ref=sum_inbox.at[me],
            send_sem=sum_send.at[step],
            recv_sem=sum_recv.at[step],
            device_id={"fsdp": peer},
            device_id_type=MESH,
        )

    def seq_link(step):
        return pltpu.make_async_remote_copy(
            src_ref=sum_mine,
            dst_ref=sum_inbox_seq.at[rank],
            send_sem=seq_send.at[step],
            recv_sem=seq_recv.at[step],
            device_id={"seq": lax.rem(rank + step, group)},
            device_id_type=MESH,
        )

    def greet(step):
        peer = lax.rem(me + step, count)
        pl.semaphore_signal(barrier, inc=1, device_id={"fsdp": peer}, device_id_type=MESH)

    def greet_seq(step):
        peer = lax.rem(rank + step, group)
        pl.semaphore_signal(barrier, inc=1, device_id={"seq": peer}, device_id_type=MESH)

    repeat(1, count, greet)
    repeat(1, group, greet_seq)

    def stage_keys(slot):
        key_raw[slot] = of_head(keys, slot)
        value_own[slot] = of_head(values, slot)

    def stage_queries(slot):
        query_raw[slot] = of_head(queries, slot)
        upstream_own[slot] = of_head(upstream, slot)

    repeat(0, heads, stage_keys)
    gain_mine[...] = jnp.zeros_like(gain_mine)
    gain_mine[0:1, 0:width] = q_gain[...]
    gain_mine[0:1, LANES : LANES + width] = k_gain[...]
    gain_inbox[pl.ds(me, 1)] = gain_mine[...][None]
    pl.semaphore_wait(barrier, count + group - 2)

    def send_keys(pair):
        for side in range(2):
            link(KEYS, side, pair).start()
            link(VALUES, side, pair).start()

    def send_queries(pair):
        for side in range(2):
            link(QUERIES, side, pair).start()
            link(UPSTREAM, side, pair).start()

    repeat(1, count, lambda step: gain_link(step).start())
    repeat(0, far_pairs, send_keys)
    repeat(0, heads, stage_queries)

    for row, ref in enumerate((queries, keys)):

        def squares(head, total):
            wide = of_head(ref, head).astype(jnp.float32)
            return total + wide * wide

        total = lax.fori_loop(0, heads, squares, jnp.zeros((rows, size), jnp.float32))
        mean = jnp.sum(total, axis=1, keepdims=True) / columns
        inverse = jnp.broadcast_to(lax.rsqrt(mean + EPS), (rows, size))
        inverse_own[row] = inverse
        inverse_out[row : row + 1, :] = jnp.transpose(inverse)[0:1, :]
    for side in range(2):
        inverse_link(side).start()

    repeat(1, count, lambda step: gain_link(step).wait())
    lane = lax.broadcasted_iota(jnp.int32, (1, LANES), 1)
    for row in range(2):
        tiles = [jnp.zeros((1, LANES), jnp.float32) for _ in range(heads + 1)]
        for owner in range(count):
            tile, offset = divmod(owner * width, LANES)
            part = gain_inbox[owner, :, row * LANES : (row + 1) * LANES]
            if offset:
                part = pltpu.roll(part, offset, 1)
            if offset + width > LANES:
                tiles[tile + 1] = tiles[tile + 1] + jnp.where(lane < offset, part, 0.0)
                part = jnp.where(lane >= offset, part, 0.0)
            tiles[tile] = tiles[tile] + part
        for head in range(heads):
            gains[row, head] = tiles[head]

    def normed(raw, inverse, row, head):
        return (raw.astype(jnp.float32) * inverse * gains[row, head]).astype(jnp.bfloat16)

    def normalise(slot):
        query_own[slot] = normed(query_raw[slot], inverse_own[0], 0, slot)
        key_own[slot] = normed(key_raw[slot], inverse_own[1], 1, slot)

    repeat(0, heads, normalise)

    key_pixel = lax.broadcasted_iota(jnp.int32, (rows, rows), 0)
    query_pixel = lax.broadcasted_iota(jnp.int32, (rows, rows), 1)
    apart_rows = jnp.abs(key_pixel // PW // TILE_H - query_pixel // PW // TILE_H)
    apart_columns = jnp.abs(key_pixel % PW // TILE_W - query_pixel % PW // TILE_W)
    apart_rows = apart_rows.astype(jnp.float32)
    apart_columns = apart_columns.astype(jnp.float32)

    def spatial(head):
        seen = (apart_rows <= limits[head, 3:4, :]) & (apart_columns <= limits[head, 4:5, :])
        return jnp.where(seen, 0.0, BLOCKED)

    def frame_bias(head, frame):
        return limits[head, frame : frame + 1, :]

    def soft(scores, bias):
        scores = scores * factor + bias
        top = jnp.maximum(jnp.max(scores, axis=0, keepdims=True), FLOOR)
        raised = jnp.exp(scores - top)
        total = jnp.maximum(jnp.sum(raised, axis=0, keepdims=True), 1e-30)
        return raised * (1.0 / total), top + jnp.log(total)

    def query_side(slot, key_all, value_all, bias, own):
        query_block, upstream_block = query_own[slot], upstream_own[slot]
        probs, logsum = soft(dot(key_all, query_block, 1, 1), bias)
        weights = probs.astype(jnp.bfloat16)
        dprobs = dot(value_all, upstream_block, 1, 1)
        deltas = jnp.sum(weights.astype(jnp.float32) * dprobs, axis=0, keepdims=True)
        dscores = (probs * (dprobs - deltas)).astype(jnp.bfloat16)
        query_grad[slot] = dot(dscores, key_all, 0, 0) * factor
        key_grad[slot] = dot(dscores[own], query_block, 1, 0) * factor
        value_grad[slot] = dot(weights[own], upstream_block, 1, 0)
        return logsum, deltas

    def alone(pair):
        for slot in (2 * pair, 2 * pair + 1):
            bias = spatial(slot) + frame_bias(slot, 1)
            query_side(slot, key_own[slot], value_own[slot], bias, slice(0, rows))

    if far_pairs < pairs:
        repeat(far_pairs, pairs, alone)

    for side in range(2):
        inverse_link(1 - side).wait_recv()
        for row in range(2):
            spread = jnp.broadcast_to(inverse_in[side, row : row + 1, :], (rows, size))
            inverse_near[side, row] = jnp.transpose(spread)

    def near_queries(pair):
        for side in range(2):
            link(KEYS, 1 - side, pair).wait_recv()
            link(VALUES, 1 - side, pair).wait_recv()
        send_queries(pair)
        for slot in (2 * pair, 2 * pair + 1):
            low = normed(key_in[0, slot], inverse_near[0, 1], 1, slot)
            high = normed(key_in[1, slot], inverse_near[1, 1], 1, slot)
            key_all = jnp.concatenate([low, key_own[slot], high], axis=0)
            value_all = jnp.concatenate([value_in[0, slot], value_own[slot], value_in[1, slot]], axis=0)
            bias = spatial(slot)
            bias = jnp.concatenate([bias + frame_bias(slot, at) for at in range(3)], axis=0)
            logsum, deltas = query_side(slot, key_all, value_all, bias, slice(rows, 2 * rows))
            stat_out[slot, 0:1, :] = logsum
            stat_out[slot, 1:2, :] = deltas
        for side in range(2):
            stat_link(side, pair).start()

    repeat(0, far_pairs, near_queries)

    def norm_back(row, ref, grad, out):
        inverse = inverse_own[row]

        def first(head, total):
            wide, slope = of_head(ref, head).astype(jnp.float32), grad[head]
            gain_rows[row, head] = jnp.sum(slope * wide * inverse, axis=0, keepdims=True)
            return total + slope * gains[row, head] * wide

        total = lax.fori_loop(0, heads, first, jnp.zeros((rows, size), jnp.float32))
        inner = jnp.sum(total, axis=1, keepdims=True) / columns
        shrink = inverse * inverse * inner

        def second(head):
            wide, slope = of_head(ref, head).astype(jnp.float32), grad[head]
            result = inverse * (slope * gains[row, head] - wide * shrink)
            out[:, pl.ds(pl.multiple_of(head * size, size), size)] = result.astype(jnp.bfloat16)

        repeat(0, heads, second)

    norm_back(0, queries, query_grad, d_queries)

    def near_keys(pair):
        for side in range(2):
            link(QUERIES, 1 - side, pair).wait_recv()
            link(UPSTREAM, 1 - side, pair).wait_recv()
            stat_link(1 - side, pair).wait_recv()
        for slot in (2 * pair, 2 * pair + 1):
            low = normed(query_in[0, slot], inverse_near[0, 0], 0, slot)
            high = normed(query_in[1, slot], inverse_near[1, 0], 0, slot)
            query_all = jnp.concatenate([low, high], axis=0)
            upstream_all = jnp.concatenate([upstream_in[0, slot], upstream_in[1, slot]], axis=0)
            bias = spatial(slot)
            bias = jnp.concatenate(
                [
                    bias + (frame_bias(slot, 0) - stat_in[0, slot, 0:1, :]),
                    bias + (frame_bias(slot, 2) - stat_in[1, slot, 0:1, :]),
                ],
                axis=1,
            )
            deltas = jnp.concatenate([stat_in[0, slot, 1:2, :], stat_in[1, slot, 1:2, :]], axis=1)
            probs = jnp.exp(dot(key_own[slot], query_all, 1, 1) * factor + bias)
            weights = probs.astype(jnp.bfloat16)
            dprobs = dot(value_own[slot], upstream_all, 1, 1)
            dscores = (probs * (dprobs - deltas)).astype(jnp.bfloat16)
            key_grad[slot] += dot(dscores, query_all, 1, 0) * factor
            value_grad[slot] += dot(weights, upstream_all, 1, 0)

    repeat(0, far_pairs, near_keys)
    norm_back(1, keys, key_grad, d_keys)

    for owner in range(count):
        tile, offset = divmod(owner * width, LANES)
        for row in range(2):
            part = gain_rows[row, tile]
            if offset:
                part = pltpu.roll(part, LANES - offset, 1)
            if offset + width > LANES:
                after = pltpu.roll(gain_rows[row, tile + 1], LANES - offset, 1)
                part = jnp.where(lane < LANES - offset, part, after)
            sum_outbox[owner, :, row * LANES : (row + 1) * LANES] = part
    sum_inbox[pl.ds(me, 1)] = sum_outbox[pl.ds(me, 1)]
    repeat(1, count, lambda step: sum_link(step).start())

    def finish_values(head):
        out = value_grad[head].astype(jnp.bfloat16)
        d_values[:, pl.ds(pl.multiple_of(head * size, size), size)] = out

    repeat(0, heads, finish_values)
    repeat(1, count, lambda step: sum_link(step).wait())
    sum_mine[...] = jnp.sum(sum_inbox[...], axis=0)
    repeat(1, group, lambda step: seq_link(step).start())
    sum_inbox_seq[pl.ds(rank, 1)] = sum_mine[...][None]

    def sent(pair):
        for side in range(2):
            for which in range(4):
                link(which, side, pair).wait_send()
            stat_link(side, pair).wait_send()

    repeat(0, far_pairs, sent)
    for side in range(2):
        inverse_link(side).wait_send()
    repeat(1, group, lambda step: seq_link(step).wait())
    total = jnp.sum(sum_inbox_seq[...], axis=0)
    d_q_gain[...] = total[:, 0:width]
    d_k_gain[...] = total[:, LANES : LANES + width]


def attention(far, identity, limits, queries, keys, values, upstream, q_gain, k_gain):
    count, group = lax.axis_size("fsdp"), lax.axis_size("seq")
    heads = limits.shape[0]
    rows, columns = queries.shape
    size = columns // heads
    width = q_gain.shape[0]
    wide, narrow = jnp.float32, jnp.bfloat16
    pairs = max(far // 2, 1)
    vmem = pl.BlockSpec(memory_space=pltpu.VMEM)
    block = (rows, size)
    dma = pltpu.SemaphoreType.DMA
    scratch = [
        pltpu.VMEM((heads,) + block, narrow),
        pltpu.VMEM((heads,) + block, narrow),
        pltpu.VMEM((heads,) + block, narrow),
        pltpu.VMEM((heads,) + block, narrow),
        pltpu.VMEM((heads,) + block, narrow),
        pltpu.VMEM((heads,) + block, narrow),
        pltpu.VMEM((2, far) + block, narrow),
        pltpu.VMEM((2, far) + block, narrow),
        pltpu.VMEM((2, far) + block, narrow),
        pltpu.VMEM((2, far) + block, narrow),
        pltpu.VMEM((far, 2, size), wide),
        pltpu.VMEM((2, far, 2, size), wide),
        pltpu.VMEM((2, size), wide),
        pltpu.VMEM((2, 2, size), wide),
        pltpu.VMEM((2,) + block, wide),
        pltpu.VMEM((2, 2) + block, wide),
        pltpu.VMEM((2, heads, 1, size), wide),
        pltpu.VMEM((2, heads, 1, size), wide),
        pltpu.VMEM((heads,) + block, wide),
        pltpu.VMEM((heads,) + block, wide),
        pltpu.VMEM((heads,) + block, wide),
        pltpu.VMEM((1, 2 * LANES), wide),
        pltpu.VMEM((count, 1, 2 * LANES), wide),
        pltpu.VMEM((count, 1, 2 * LANES), wide),
        pltpu.VMEM((count, 1, 2 * LANES), wide),
        pltpu.VMEM((1, 2 * LANES), wide),
        pltpu.VMEM((group, 1, 2 * LANES), wide),
        dma((4, 2, pairs)),
        dma((4, 2, pairs)),
        dma((2, pairs)),
        dma((2, pairs)),
        dma((2,)),
        dma((2,)),
        dma((count,)),
        dma((count,)),
        dma((count,)),
        dma((count,)),
        dma((group,)),
        dma((group,)),
    ]
    d_queries, d_keys, d_values, d_q_gain, d_k_gain = pl.pallas_call(
        functools.partial(attention_kernel, far, count, group),
        out_shape=[jax.ShapeDtypeStruct((rows, columns), narrow)] * 3
        + [jax.ShapeDtypeStruct((1, width), wide)] * 2,
        in_specs=[vmem] * 7,
        out_specs=[vmem] * 5,
        scratch_shapes=scratch,
        compiler_params=pltpu.CompilerParams(
            collective_id=identity, has_side_effects=True, vmem_limit_bytes=48 * 1024 * 1024
        ),
        name="attention_backward",
    )(limits, queries, keys, values, upstream, q_gain[None], k_gain[None])
    return d_queries, d_keys, d_values, d_q_gain[0], d_k_gain[0]


def head_limits(windows, frames):
    rank, group = lax.axis_index("seq"), lax.axis_size("seq")
    near = windows[:, 0] >= 1
    own = jnp.full_like(near, rank < frames)
    below = near & (rank > 0) & (rank < frames)
    above = near & (rank + 1 < group) & (rank + 1 < frames)
    blocks = jnp.where(jnp.stack([below, own, above], 1), 0.0, BLOCKED)
    table = jnp.concatenate([blocks, windows.astype(jnp.float32)[:, 1:], jnp.zeros_like(blocks)], 1)
    return jnp.broadcast_to(table[:, :, None], table.shape + (LANES,))


def local(queries, keys, values, grad_out, q_gain, k_gain, lengths, windows):
    shape = queries.shape
    flat = (shape[1] * shape[2], shape[3])
    arrays = [array.reshape(flat) for array in (queries, keys, values, grad_out)]
    limits = head_limits(windows, lengths[0])
    heads = windows.shape[0]
    d_queries, d_keys, d_values, d_q_gain, d_k_gain = attention(
        heads, 0, limits, *arrays, q_gain, k_gain
    )
    return (
        d_queries.reshape(shape),
        d_keys.reshape(shape),
        d_values.reshape(shape),
        d_q_gain,
        d_k_gain,
    )


def solution(mesh):
    in_specs = (
        P("fsdp", "seq", None, None),
        P("fsdp", "seq", None, None),
        P("fsdp", "seq", None, None),
        P("fsdp", "seq", None, None),
        P("fsdp"),
        P("fsdp"),
        P("fsdp"),
        P(),
    )
    out_specs = (
        P("fsdp", "seq", None, None),
        P("fsdp", "seq", None, None),
        P("fsdp", "seq", None, None),
        P("fsdp"),
        P("fsdp"),
    )
    return jax.shard_map(local, mesh=mesh, in_specs=in_specs, out_specs=out_specs, check_vma=False)
```

```python
import functools

import jax
import jax.numpy as jnp
from jax import lax
from jax.experimental import pallas as pl
from jax.experimental.pallas import tpu as pltpu
from jax.sharding import PartitionSpec as P

PW = 8
TILE_H = 4
TILE_W = 4
LANES = 128
EPS = 1e-06
BLOCKED = -1e30
FLOOR = -1e29
MESH = pl.DeviceIdType.MESH
KEYS, VALUES, QUERIES, UPSTREAM = range(4)
CAPACITIES = (6, 8, 10, 12, 14, 16, 20)


def dot(left, right, left_dim, right_dim):
    return lax.dot_general(
        left, right, (((left_dim,), (right_dim,)), ((), ())), preferred_element_type=jnp.float32
    )


def attention_kernel(
    far,
    count,
    group,
    perm,
    place,
    limits,
    queries_hbm,
    keys_hbm,
    values_hbm,
    upstream_hbm,
    q_gain,
    k_gain,
    d_queries,
    d_keys,
    d_values,
    d_q_gain,
    d_k_gain,
    keys,
    values,
    queries,
    upstream,
    key_raw,
    query_raw,
    key_own,
    query_own,
    value_own,
    upstream_own,
    key_in,
    value_in,
    query_in,
    upstream_in,
    stat_out,
    stat_in,
    inverse_out,
    inverse_in,
    inverse_own,
    inverse_near,
    gains,
    gain_rows,
    query_grad,
    key_grad,
    value_grad,
    gain_mine,
    gain_inbox,
    sum_outbox,
    sum_inbox,
    sum_mine,
    sum_inbox_seq,
    load_sem,
    send_sem,
    recv_sem,
    stat_send,
    stat_recv,
    inverse_send,
    inverse_recv,
    gain_send,
    gain_recv,
    sum_send,
    sum_recv,
    seq_send,
    seq_recv,
):
    me = lax.axis_index("fsdp")
    rank = lax.axis_index("seq")
    heads = limits.shape[0]
    rows, columns = queries_hbm.shape
    size = columns // heads
    width = q_gain.shape[1]
    factor = size ** (-0.5)
    far_pairs, pairs = far // 2, heads // 2
    below, above = lax.rem(rank + group - 1, group), lax.rem(rank + 1, group)
    barrier = pltpu.get_barrier_semaphore()

    def repeat(first, last, body):
        lax.fori_loop(first, last, lambda step, carry: (body(step), carry)[1], 0)

    arrays = ((keys_hbm, keys), (values_hbm, values), (queries_hbm, queries), (upstream_hbm, upstream))

    def load(which, head):
        source, target = arrays[which]
        part = pl.ds(pl.multiple_of(head * size, size), size)
        return pltpu.make_async_copy(source.at[:, part], target.at[head], load_sem.at[which, head])

    outgoing = (key_raw, value_own, query_raw, upstream_own)
    incoming = (key_in, value_in, query_in, upstream_in)

    def link(which, side, pair):
        part = pl.ds(2 * pair, 2)
        return pltpu.make_async_remote_copy(
            src_ref=outgoing[which].at[part],
            dst_ref=incoming[which].at[1 - side, part],
            send_sem=send_sem.at[which, side, pair],
            recv_sem=recv_sem.at[which, 1 - side, pair],
            device_id={"seq": above if side else below},
            device_id_type=MESH,
        )

    def stat_link(side, pair):
        part = pl.ds(2 * pair, 2)
        return pltpu.make_async_remote_copy(
            src_ref=stat_out.at[part],
            dst_ref=stat_in.at[1 - side, part],
            send_sem=stat_send.at[side, pair],
            recv_sem=stat_recv.at[1 - side, pair],
            device_id={"seq": above if side else below},
            device_id_type=MESH,
        )

    def inverse_link(side):
        return pltpu.make_async_remote_copy(
            src_ref=inverse_out,
            dst_ref=inverse_in.at[1 - side],
            send_sem=inverse_send.at[side],
            recv_sem=inverse_recv.at[1 - side],
            device_id={"seq": above if side else below},
            device_id_type=MESH,
        )

    def gain_link(step):
        return pltpu.make_async_remote_copy(
            src_ref=gain_mine,
            dst_ref=gain_inbox.at[me],
            send_sem=gain_send.at[step],
            recv_sem=gain_recv.at[step],
            device_id={"fsdp": lax.rem(me + step, count)},
            device_id_type=MESH,
        )

    def sum_link(step):
        peer = lax.rem(me + step, count)
        return pltpu.make_async_remote_copy(
            src_ref=sum_outbox.at[peer],
            dst_ref=sum_inbox.at[me],
            send_sem=sum_send.at[step],
            recv_sem=sum_recv.at[step],
            device_id={"fsdp": peer},
            device_id_type=MESH,
        )

    def seq_link(step):
        return pltpu.make_async_remote_copy(
            src_ref=sum_mine,
            dst_ref=sum_inbox_seq.at[rank],
            send_sem=seq_send.at[step],
            recv_sem=seq_recv.at[step],
            device_id={"seq": lax.rem(rank + step, group)},
            device_id_type=MESH,
        )

    def greet(step):
        peer = lax.rem(me + step, count)
        pl.semaphore_signal(barrier, inc=1, device_id={"fsdp": peer}, device_id_type=MESH)

    def greet_seq(step):
        peer = lax.rem(rank + step, group)
        pl.semaphore_signal(barrier, inc=1, device_id={"seq": peer}, device_id_type=MESH)

    repeat(1, count, greet)
    repeat(1, group, greet_seq)
    for which in range(4):
        repeat(0, heads, lambda head: load(which, head).start())
    gain_mine[...] = jnp.zeros_like(gain_mine)
    gain_mine[0:1, 0:width] = q_gain[...]
    gain_mine[0:1, LANES : LANES + width] = k_gain[...]
    gain_inbox[pl.ds(me, 1)] = gain_mine[...][None]

    def stage_keys(slot):
        key_raw[slot] = keys[perm[slot]]

    def stage_values(slot):
        value_own[slot] = values[perm[slot]]

    def stage_queries(slot):
        query_raw[slot] = queries[perm[slot]]

    def stage_upstream(slot):
        upstream_own[slot] = upstream[perm[slot]]

    def invert(row, ref):
        def squares(head, total):
            wide = ref[head].astype(jnp.float32)
            return total + wide * wide

        total = lax.fori_loop(0, heads, squares, jnp.zeros((rows, size), jnp.float32))
        mean = jnp.sum(total, axis=1, keepdims=True) / columns
        inverse = jnp.broadcast_to(lax.rsqrt(mean + EPS), (rows, size))
        inverse_own[row] = inverse
        inverse_out[row : row + 1, :] = jnp.transpose(inverse)[0:1, :]

    repeat(0, heads, lambda head: load(KEYS, head).wait())
    repeat(0, far, stage_keys)
    repeat(0, heads, lambda head: load(VALUES, head).wait())
    repeat(0, heads, stage_values)
    invert(1, keys)
    repeat(0, heads, lambda head: load(QUERIES, head).wait())
    invert(0, queries)
    repeat(0, far, stage_queries)
    repeat(0, heads, lambda head: load(UPSTREAM, head).wait())
    repeat(0, heads, stage_upstream)
    pl.semaphore_wait(barrier, count + group - 2)

    def send_keys(pair):
        for side in range(2):
            link(KEYS, side, pair).start()
            link(VALUES, side, pair).start()

    def send_queries(pair):
        for side in range(2):
            link(QUERIES, side, pair).start()
            link(UPSTREAM, side, pair).start()

    for side in range(2):
        inverse_link(side).start()
    repeat(1, count, lambda step: gain_link(step).start())
    repeat(0, far_pairs, send_keys)

    repeat(1, count, lambda step: gain_link(step).wait())
    lane = lax.broadcasted_iota(jnp.int32, (1, LANES), 1)
    for row in range(2):
        tiles = [jnp.zeros((1, LANES), jnp.float32) for _ in range(heads + 1)]
        for owner in range(count):
            tile, offset = divmod(owner * width, LANES)
            part = gain_inbox[owner, :, row * LANES : (row + 1) * LANES]
            if offset:
                part = pltpu.roll(part, offset, 1)
            if offset + width > LANES:
                tiles[tile + 1] = tiles[tile + 1] + jnp.where(lane < offset, part, 0.0)
                part = jnp.where(lane >= offset, part, 0.0)
            tiles[tile] = tiles[tile] + part
        for head in range(heads):
            gains[row, head] = tiles[head]

    def normed(raw, inverse, row, head):
        return (raw.astype(jnp.float32) * inverse * gains[row, head]).astype(jnp.bfloat16)

    def normalise(slot):
        head = perm[slot]
        query_own[slot] = normed(queries[head], inverse_own[0], 0, head)
        key_own[slot] = normed(keys[head], inverse_own[1], 1, head)

    repeat(0, heads, normalise)

    key_pixel = lax.broadcasted_iota(jnp.int32, (rows, rows), 0)
    query_pixel = lax.broadcasted_iota(jnp.int32, (rows, rows), 1)
    apart_rows = jnp.abs(key_pixel // PW // TILE_H - query_pixel // PW // TILE_H)
    apart_columns = jnp.abs(key_pixel % PW // TILE_W - query_pixel % PW // TILE_W)
    apart_rows = apart_rows.astype(jnp.float32)
    apart_columns = apart_columns.astype(jnp.float32)

    def spatial(head):
        seen = (apart_rows <= limits[head, 3:4, :]) & (apart_columns <= limits[head, 4:5, :])
        return jnp.where(seen, 0.0, BLOCKED)

    def frame_bias(head, frame):
        return limits[head, frame : frame + 1, :]

    def soft(scores, bias):
        scores = scores * factor + bias
        top = jnp.maximum(jnp.max(scores, axis=0, keepdims=True), FLOOR)
        raised = jnp.exp(scores - top)
        total = jnp.maximum(jnp.sum(raised, axis=0, keepdims=True), 1e-30)
        return raised * (1.0 / total), top + jnp.log(total)

    def query_side(slot, key_all, value_all, bias, own):
        query_block, upstream_block = query_own[slot], upstream_own[slot]
        probs, logsum = soft(dot(key_all, query_block, 1, 1), bias)
        weights = probs.astype(jnp.bfloat16)
        dprobs = dot(value_all, upstream_block, 1, 1)
        deltas = jnp.sum(weights.astype(jnp.float32) * dprobs, axis=0, keepdims=True)
        dscores = (probs * (dprobs - deltas)).astype(jnp.bfloat16)
        query_grad[slot] = dot(dscores, key_all, 0, 0) * factor
        key_grad[slot] = dot(dscores[own], query_block, 1, 0) * factor
        value_grad[slot] = dot(weights[own], upstream_block, 1, 0)
        return logsum, deltas

    def alone(pair):
        for slot in (2 * pair, 2 * pair + 1):
            bias = spatial(slot) + frame_bias(slot, 1)
            query_side(slot, key_own[slot], value_own[slot], bias, slice(0, rows))

    if far_pairs < pairs:
        repeat(far_pairs, pairs, alone)

    for side in range(2):
        inverse_link(1 - side).wait_recv()
        for row in range(2):
            spread = jnp.broadcast_to(inverse_in[side, row : row + 1, :], (rows, size))
            inverse_near[side, row] = jnp.transpose(spread)

    def near_queries(pair):
        for side in range(2):
            link(KEYS, 1 - side, pair).wait_recv()
            link(VALUES, 1 - side, pair).wait_recv()
        send_queries(pair)
        for slot in (2 * pair, 2 * pair + 1):
            head = perm[slot]
            low = normed(key_in[0, slot], inverse_near[0, 1], 1, head)
            high = normed(key_in[1, slot], inverse_near[1, 1], 1, head)
            key_all = jnp.concatenate([low, key_own[slot], high], axis=0)
            value_all = jnp.concatenate([value_in[0, slot], value_own[slot], value_in[1, slot]], axis=0)
            bias = spatial(slot)
            bias = jnp.concatenate([bias + frame_bias(slot, at) for at in range(3)], axis=0)
            logsum, deltas = query_side(slot, key_all, value_all, bias, slice(rows, 2 * rows))
            stat_out[slot, 0:1, :] = logsum
            stat_out[slot, 1:2, :] = deltas
        for side in range(2):
            stat_link(side, pair).start()

    repeat(0, far_pairs, near_queries)

    def norm_back(row, ref, grad, out):
        inverse = inverse_own[row]

        def first(head, total):
            wide, slope = ref[head].astype(jnp.float32), grad[place[head]]
            gain_rows[row, head] = jnp.sum(slope * wide * inverse, axis=0, keepdims=True)
            return total + slope * gains[row, head] * wide

        total = lax.fori_loop(0, heads, first, jnp.zeros((rows, size), jnp.float32))
        inner = jnp.sum(total, axis=1, keepdims=True) / columns
        shrink = inverse * inverse * inner

        def second(head):
            wide, slope = ref[head].astype(jnp.float32), grad[place[head]]
            result = inverse * (slope * gains[row, head] - wide * shrink)
            out[:, pl.ds(pl.multiple_of(head * size, size), size)] = result.astype(jnp.bfloat16)

        repeat(0, heads, second)

    norm_back(0, queries, query_grad, d_queries)

    def near_keys(pair):
        for side in range(2):
            link(QUERIES, 1 - side, pair).wait_recv()
            link(UPSTREAM, 1 - side, pair).wait_recv()
            stat_link(1 - side, pair).wait_recv()
        for slot in (2 * pair, 2 * pair + 1):
            head = perm[slot]
            low = normed(query_in[0, slot], inverse_near[0, 0], 0, head)
            high = normed(query_in[1, slot], inverse_near[1, 0], 0, head)
            query_all = jnp.concatenate([low, high], axis=0)
            upstream_all = jnp.concatenate([upstream_in[0, slot], upstream_in[1, slot]], axis=0)
            bias = spatial(slot)
            bias = jnp.concatenate(
                [
                    bias + (frame_bias(slot, 0) - stat_in[0, slot, 0:1, :]),
                    bias + (frame_bias(slot, 2) - stat_in[1, slot, 0:1, :]),
                ],
                axis=1,
            )
            deltas = jnp.concatenate([stat_in[0, slot, 1:2, :], stat_in[1, slot, 1:2, :]], axis=1)
            probs = jnp.exp(dot(key_own[slot], query_all, 1, 1) * factor + bias)
            weights = probs.astype(jnp.bfloat16)
            dprobs = dot(value_own[slot], upstream_all, 1, 1)
            dscores = (probs * (dprobs - deltas)).astype(jnp.bfloat16)
            key_grad[slot] += dot(dscores, query_all, 1, 0) * factor
            value_grad[slot] += dot(weights, upstream_all, 1, 0)

    repeat(0, far_pairs, near_keys)
    norm_back(1, keys, key_grad, d_keys)

    for owner in range(count):
        tile, offset = divmod(owner * width, LANES)
        for row in range(2):
            part = gain_rows[row, tile]
            if offset:
                part = pltpu.roll(part, LANES - offset, 1)
            if offset + width > LANES:
                after = pltpu.roll(gain_rows[row, tile + 1], LANES - offset, 1)
                part = jnp.where(lane < LANES - offset, part, after)
            sum_outbox[owner, :, row * LANES : (row + 1) * LANES] = part
    sum_inbox[pl.ds(me, 1)] = sum_outbox[pl.ds(me, 1)]
    repeat(1, count, lambda step: sum_link(step).start())

    def finish_values(head):
        out = value_grad[place[head]].astype(jnp.bfloat16)
        d_values[:, pl.ds(pl.multiple_of(head * size, size), size)] = out

    repeat(0, heads, finish_values)
    repeat(1, count, lambda step: sum_link(step).wait())
    sum_mine[...] = jnp.sum(sum_inbox[...], axis=0)
    repeat(1, group, lambda step: seq_link(step).start())
    sum_inbox_seq[pl.ds(rank, 1)] = sum_mine[...][None]

    def sent(pair):
        for side in range(2):
            for which in range(4):
                link(which, side, pair).wait_send()
            stat_link(side, pair).wait_send()

    repeat(0, far_pairs, sent)
    for side in range(2):
        inverse_link(side).wait_send()
    repeat(1, group, lambda step: seq_link(step).wait())
    total = jnp.sum(sum_inbox_seq[...], axis=0)
    d_q_gain[...] = total[:, 0:width]
    d_k_gain[...] = total[:, LANES : LANES + width]


def attention(far, identity, perm, place, limits, queries, keys, values, upstream, q_gain, k_gain):
    count, group = lax.axis_size("fsdp"), lax.axis_size("seq")
    heads = limits.shape[0]
    rows, columns = queries.shape
    size = columns // heads
    width = q_gain.shape[0]
    wide, narrow = jnp.float32, jnp.bfloat16
    pairs = far // 2
    smem = pl.BlockSpec(memory_space=pltpu.SMEM)
    hbm = pl.BlockSpec(memory_space=pl.ANY)
    vmem = pl.BlockSpec(memory_space=pltpu.VMEM)
    block = (rows, size)
    dma = pltpu.SemaphoreType.DMA
    scratch = [
        pltpu.VMEM((heads,) + block, narrow),
        pltpu.VMEM((heads,) + block, narrow),
        pltpu.VMEM((heads,) + block, narrow),
        pltpu.VMEM((heads,) + block, narrow),
        pltpu.VMEM((far,) + block, narrow),
        pltpu.VMEM((far,) + block, narrow),
        pltpu.VMEM((heads,) + block, narrow),
        pltpu.VMEM((heads,) + block, narrow),
        pltpu.VMEM((heads,) + block, narrow),
        pltpu.VMEM((heads,) + block, narrow),
        pltpu.VMEM((2, far) + block, narrow),
        pltpu.VMEM((2, far) + block, narrow),
        pltpu.VMEM((2, far) + block, narrow),
        pltpu.VMEM((2, far) + block, narrow),
        pltpu.VMEM((far, 2, size), wide),
        pltpu.VMEM((2, far, 2, size), wide),
        pltpu.VMEM((2, size), wide),
        pltpu.VMEM((2, 2, size), wide),
        pltpu.VMEM((2,) + block, wide),
        pltpu.VMEM((2, 2) + block, wide),
        pltpu.VMEM((2, heads, 1, size), wide),
        pltpu.VMEM((2, heads, 1, size), wide),
        pltpu.VMEM((heads,) + block, wide),
        pltpu.VMEM((heads,) + block, wide),
        pltpu.VMEM((heads,) + block, wide),
        pltpu.VMEM((1, 2 * LANES), wide),
        pltpu.VMEM((count, 1, 2 * LANES), wide),
        pltpu.VMEM((count, 1, 2 * LANES), wide),
        pltpu.VMEM((count, 1, 2 * LANES), wide),
        pltpu.VMEM((1, 2 * LANES), wide),
        pltpu.VMEM((group, 1, 2 * LANES), wide),
        dma((4, heads)),
        dma((4, 2, pairs)),
        dma((4, 2, pairs)),
        dma((2, pairs)),
        dma((2, pairs)),
        dma((2,)),
        dma((2,)),
        dma((count,)),
        dma((count,)),
        dma((count,)),
        dma((count,)),
        dma((group,)),
        dma((group,)),
    ]
    d_queries, d_keys, d_values, d_q_gain, d_k_gain = pl.pallas_call(
        functools.partial(attention_kernel, far, count, group),
        out_shape=[jax.ShapeDtypeStruct((rows, columns), narrow)] * 3
        + [jax.ShapeDtypeStruct((1, width), wide)] * 2,
        in_specs=[smem] * 2 + [vmem] + [hbm] * 4 + [vmem] * 2,
        out_specs=[vmem] * 5,
        scratch_shapes=scratch,
        compiler_params=pltpu.CompilerParams(
            collective_id=identity, has_side_effects=True, vmem_limit_bytes=56 * 1024 * 1024
        ),
        name="attention_backward",
    )(perm, place, limits, queries, keys, values, upstream, q_gain[None], k_gain[None])
    return d_queries, d_keys, d_values, d_q_gain[0], d_k_gain[0]


def head_order(windows, frames):
    rank, group = lax.axis_index("seq"), lax.axis_size("seq")
    heads = windows.shape[0]
    near = windows[:, 0] >= 1
    ahead = jnp.arange(heads)[None, :] < jnp.arange(heads)[:, None]
    before = jnp.where(near[:, None], near[None, :] & ahead, near[None, :] | ahead)
    place = jnp.sum(before.astype(jnp.int32), 1)
    here = place[None, :] == jnp.arange(heads)[:, None]
    perm = jnp.sum(jnp.where(here, jnp.arange(heads, dtype=jnp.int32)[None, :], 0), 1)
    own = jnp.full_like(near, rank < frames)
    below = near & (rank > 0) & (rank < frames)
    above = near & (rank + 1 < group) & (rank + 1 < frames)
    blocks = jnp.where(jnp.stack([below, own, above], 1), 0.0, BLOCKED)
    table = jnp.concatenate([blocks, windows.astype(jnp.float32)[:, 1:], jnp.zeros_like(blocks)], 1)
    table = jnp.sum(jnp.where(here[:, :, None], table[None], 0.0), 1)
    limits = jnp.broadcast_to(table[:, :, None], table.shape + (LANES,))
    return perm, place, limits, jnp.sum(near.astype(jnp.int32))


def local(queries, keys, values, grad_out, q_gain, k_gain, lengths, windows):
    shape = queries.shape
    flat = (shape[1] * shape[2], shape[3])
    arrays = [array.reshape(flat) for array in (queries, keys, values, grad_out)]
    perm, place, limits, near = head_order(windows, lengths[0])
    heads = windows.shape[0]
    capacities = [at for at in CAPACITIES if at < heads] + [heads]
    branch = sum((near > at).astype(jnp.int32) for at in capacities[:-1])
    d_queries, d_keys, d_values, d_q_gain, d_k_gain = lax.switch(
        branch,
        [functools.partial(attention, far, at) for at, far in enumerate(capacities)],
        perm,
        place,
        limits,
        *arrays,
        q_gain,
        k_gain,
    )
    return (
        d_queries.reshape(shape),
        d_keys.reshape(shape),
        d_values.reshape(shape),
        d_q_gain,
        d_k_gain,
    )


def solution(mesh):
    in_specs = (
        P("fsdp", "seq", None, None),
        P("fsdp", "seq", None, None),
        P("fsdp", "seq", None, None),
        P("fsdp", "seq", None, None),
        P("fsdp"),
        P("fsdp"),
        P("fsdp"),
        P(),
    )
    out_specs = (
        P("fsdp", "seq", None, None),
        P("fsdp", "seq", None, None),
        P("fsdp", "seq", None, None),
        P("fsdp"),
        P("fsdp"),
    )
    return jax.shard_map(local, mesh=mesh, in_specs=in_specs, out_specs=out_specs, check_vma=False)
```

```python
import functools

import jax
import jax.numpy as jnp
from jax import lax
from jax.experimental import pallas as pl
from jax.experimental.pallas import tpu as pltpu
from jax.sharding import PartitionSpec as P

PW = 8
TILE_H = 4
TILE_W = 4
LANES = 128
EPS = 1e-06
BLOCKED = -1e30
FLOOR = -1e29
MESH = pl.DeviceIdType.MESH
KEYS, VALUES, QUERIES, UPSTREAM = range(4)
CAPACITIES = (6, 8, 10, 12, 14, 16, 20)


def dot(left, right, left_dim, right_dim):
    return lax.dot_general(
        left, right, (((left_dim,), (right_dim,)), ((), ())), preferred_element_type=jnp.float32
    )


def attention_kernel(
    far,
    count,
    group,
    perm,
    place,
    limits,
    queries_hbm,
    keys_hbm,
    values_hbm,
    upstream_hbm,
    q_gain,
    k_gain,
    d_queries,
    d_keys,
    d_values,
    d_gains,
    keys,
    values,
    queries,
    upstream,
    key_raw,
    query_raw,
    key_own,
    query_own,
    value_own,
    upstream_own,
    key_in,
    value_in,
    query_in,
    upstream_in,
    stat_out,
    stat_in,
    inverse_out,
    inverse_in,
    inverse_own,
    inverse_near,
    shrink,
    gains,
    gain_rows,
    query_grad,
    key_grad,
    value_grad,
    gain_mine,
    gain_inbox,
    sum_outbox,
    sum_inbox,
    sum_mine,
    sum_inbox_seq,
    load_sem,
    send_sem,
    recv_sem,
    stat_send,
    stat_recv,
    inverse_send,
    inverse_recv,
    gain_send,
    gain_recv,
    sum_send,
    sum_recv,
    seq_send,
    seq_recv,
):
    me = lax.axis_index("fsdp")
    rank = lax.axis_index("seq")
    heads = limits.shape[0]
    rows, columns = queries_hbm.shape
    size = columns // heads
    width = q_gain.shape[1]
    factor = size ** (-0.5)
    far_pairs, pairs = far // 2, heads // 2
    below, above = lax.rem(rank + group - 1, group), lax.rem(rank + 1, group)
    barrier = pltpu.get_barrier_semaphore()

    def farthest(step):
        return count // 2 + (1 - 2 * (step % 2)) * ((step + 1) // 2)

    def repeat(first, last, body):
        lax.fori_loop(first, last, lambda step, carry: (body(step), carry)[1], 0)

    arrays = ((keys_hbm, keys), (values_hbm, values), (queries_hbm, queries), (upstream_hbm, upstream))

    def load(which, head):
        source, target = arrays[which]
        part = pl.ds(pl.multiple_of(head * size, size), size)
        return pltpu.make_async_copy(source.at[:, part], target.at[head], load_sem.at[which, head])

    outgoing = (key_raw, value_own, query_raw, upstream_own)
    incoming = (key_in, value_in, query_in, upstream_in)

    def link(which, side, pair):
        part = pl.ds(2 * pair, 2)
        return pltpu.make_async_remote_copy(
            src_ref=outgoing[which].at[part],
            dst_ref=incoming[which].at[1 - side, part],
            send_sem=send_sem.at[which, side, pair],
            recv_sem=recv_sem.at[which, 1 - side, pair],
            device_id={"seq": above if side else below},
            device_id_type=MESH,
        )

    def stat_link(side, pair):
        part = pl.ds(2 * pair, 2)
        return pltpu.make_async_remote_copy(
            src_ref=stat_out.at[part],
            dst_ref=stat_in.at[1 - side, part],
            send_sem=stat_send.at[side, pair],
            recv_sem=stat_recv.at[1 - side, pair],
            device_id={"seq": above if side else below},
            device_id_type=MESH,
        )

    def inverse_link(side):
        return pltpu.make_async_remote_copy(
            src_ref=inverse_out,
            dst_ref=inverse_in.at[1 - side],
            send_sem=inverse_send.at[side],
            recv_sem=inverse_recv.at[1 - side],
            device_id={"seq": above if side else below},
            device_id_type=MESH,
        )

    def gain_link(step):
        step = farthest(step)
        return pltpu.make_async_remote_copy(
            src_ref=gain_mine,
            dst_ref=gain_inbox.at[me],
            send_sem=gain_send.at[step],
            recv_sem=gain_recv.at[step],
            device_id={"fsdp": lax.rem(me + step, count)},
            device_id_type=MESH,
        )

    def sum_link(step):
        step = farthest(step)
        peer = lax.rem(me + step, count)
        return pltpu.make_async_remote_copy(
            src_ref=sum_outbox.at[peer],
            dst_ref=sum_inbox.at[me],
            send_sem=sum_send.at[step],
            recv_sem=sum_recv.at[step],
            device_id={"fsdp": peer},
            device_id_type=MESH,
        )

    def seq_link(step):
        return pltpu.make_async_remote_copy(
            src_ref=sum_mine,
            dst_ref=sum_inbox_seq.at[rank],
            send_sem=seq_send.at[step],
            recv_sem=seq_recv.at[step],
            device_id={"seq": lax.rem(rank + step, group)},
            device_id_type=MESH,
        )

    def greet(step):
        peer = lax.rem(me + farthest(step), count)
        pl.semaphore_signal(barrier, inc=1, device_id={"fsdp": peer}, device_id_type=MESH)

    def greet_seq(step):
        peer = lax.rem(rank + step, group)
        pl.semaphore_signal(barrier, inc=1, device_id={"seq": peer}, device_id_type=MESH)

    repeat(0, count - 1, greet)
    repeat(1, group, greet_seq)
    for which in range(4):
        repeat(0, heads, lambda head: load(which, head).start())
    gain_mine[...] = jnp.zeros_like(gain_mine)
    gain_mine[0:1, 0:width] = q_gain[...]
    gain_mine[0:1, LANES : LANES + width] = k_gain[...]
    gain_inbox[pl.ds(me, 1)] = gain_mine[...][None]

    def stage_keys(slot):
        key_raw[slot] = keys[perm[slot]]

    def stage_values(slot):
        value_own[slot] = values[perm[slot]]

    def stage_queries(slot):
        query_raw[slot] = queries[perm[slot]]

    def stage_upstream(slot):
        upstream_own[slot] = upstream[perm[slot]]

    def invert(row, ref):
        def squares(head, total):
            wide = ref[head].astype(jnp.float32)
            return total + wide * wide

        total = lax.fori_loop(0, heads, squares, jnp.zeros((rows, size), jnp.float32))
        mean = jnp.sum(total, axis=1, keepdims=True) / columns
        inverse = jnp.broadcast_to(lax.rsqrt(mean + EPS), (rows, size))
        inverse_own[row] = inverse
        inverse_out[row : row + 1, :] = jnp.transpose(inverse)[0:1, :]

    repeat(0, heads, lambda head: load(KEYS, head).wait())
    repeat(0, far, stage_keys)
    repeat(0, heads, lambda head: load(VALUES, head).wait())
    repeat(0, heads, stage_values)
    invert(1, keys)
    repeat(0, heads, lambda head: load(QUERIES, head).wait())
    invert(0, queries)
    repeat(0, far, stage_queries)
    repeat(0, heads, lambda head: load(UPSTREAM, head).wait())
    repeat(0, heads, stage_upstream)
    pl.semaphore_wait(barrier, count + group - 2)

    def send_keys(pair):
        for side in range(2):
            link(KEYS, side, pair).start()
            link(VALUES, side, pair).start()

    def send_queries(pair):
        for side in range(2):
            link(QUERIES, side, pair).start()
            link(UPSTREAM, side, pair).start()

    for side in range(2):
        inverse_link(side).start()
    repeat(0, 1, send_keys)
    repeat(0, count - 1, lambda step: gain_link(step).start())
    repeat(1, far_pairs, send_keys)

    repeat(0, count - 1, lambda step: gain_link(step).wait())
    lane = lax.broadcasted_iota(jnp.int32, (1, LANES), 1)
    for row in range(2):
        tiles = [jnp.zeros((1, LANES), jnp.float32) for _ in range(heads + 1)]
        for owner in range(count):
            tile, offset = divmod(owner * width, LANES)
            part = gain_inbox[owner, :, row * LANES : (row + 1) * LANES]
            if offset:
                part = pltpu.roll(part, offset, 1)
            if offset + width > LANES:
                tiles[tile + 1] = tiles[tile + 1] + jnp.where(lane < offset, part, 0.0)
                part = jnp.where(lane >= offset, part, 0.0)
            tiles[tile] = tiles[tile] + part
        for head in range(heads):
            gains[row, head] = tiles[head]

    def normed(raw, inverse, row, head):
        return (raw.astype(jnp.float32) * inverse * gains[row, head]).astype(jnp.bfloat16)

    def normalise(slot):
        head = perm[slot]
        query_own[slot] = normed(queries[head], inverse_own[0], 0, head)
        key_own[slot] = normed(keys[head], inverse_own[1], 1, head)

    repeat(0, heads, normalise)

    key_pixel = lax.broadcasted_iota(jnp.int32, (rows, rows), 0)
    query_pixel = lax.broadcasted_iota(jnp.int32, (rows, rows), 1)
    apart_rows = jnp.abs(key_pixel // PW // TILE_H - query_pixel // PW // TILE_H)
    apart_columns = jnp.abs(key_pixel % PW // TILE_W - query_pixel % PW // TILE_W)
    apart_rows = apart_rows.astype(jnp.float32)
    apart_columns = apart_columns.astype(jnp.float32)

    def spatial(head):
        seen = (apart_rows <= limits[head, 3:4, :]) & (apart_columns <= limits[head, 4:5, :])
        return jnp.where(seen, 0.0, BLOCKED)

    def frame_bias(head, frame):
        return limits[head, frame : frame + 1, :]

    def soft(scores, bias):
        scores = scores * factor + bias
        top = jnp.maximum(jnp.max(scores, axis=0, keepdims=True), FLOOR)
        raised = jnp.exp(scores - top)
        total = jnp.maximum(jnp.sum(raised, axis=0, keepdims=True), 1e-30)
        return raised * (1.0 / total), top + jnp.log(total)

    def query_side(slot, key_all, value_all, bias, own):
        query_block, upstream_block = query_own[slot], upstream_own[slot]
        probs, logsum = soft(dot(key_all, query_block, 1, 1), bias)
        weights = probs.astype(jnp.bfloat16)
        dprobs = dot(value_all, upstream_block, 1, 1)
        deltas = jnp.sum(weights.astype(jnp.float32) * dprobs, axis=0, keepdims=True)
        dscores = (probs * (dprobs - deltas)).astype(jnp.bfloat16)
        query_grad[slot] = dot(dscores, key_all, 0, 0) * factor
        key_grad[slot] = dot(dscores[own], query_block, 1, 0) * factor
        value_grad[slot] = dot(weights[own], upstream_block, 1, 0)
        return logsum, deltas

    def alone(pair):
        for slot in (2 * pair, 2 * pair + 1):
            bias = spatial(slot) + frame_bias(slot, 1)
            query_side(slot, key_own[slot], value_own[slot], bias, slice(0, rows))

    early = far_pairs // 2
    repeat(0, early, send_queries)
    if far_pairs < pairs:
        repeat(far_pairs, pairs, alone)

    for side in range(2):
        inverse_link(1 - side).wait_recv()
        for row in range(2):
            spread = jnp.broadcast_to(inverse_in[side, row : row + 1, :], (rows, size))
            inverse_near[side, row] = jnp.transpose(spread)

    def near_queries(pair, send_queries_after):
        for side in range(2):
            link(KEYS, 1 - side, pair).wait_recv()
            link(VALUES, 1 - side, pair).wait_recv()
        send_queries_after(pair)
        for slot in (2 * pair, 2 * pair + 1):
            head = perm[slot]
            low = normed(key_in[0, slot], inverse_near[0, 1], 1, head)
            high = normed(key_in[1, slot], inverse_near[1, 1], 1, head)
            key_all = jnp.concatenate([low, key_own[slot], high], axis=0)
            value_all = jnp.concatenate([value_in[0, slot], value_own[slot], value_in[1, slot]], axis=0)
            bias = spatial(slot)
            bias = jnp.concatenate([bias + frame_bias(slot, at) for at in range(3)], axis=0)
            logsum, deltas = query_side(slot, key_all, value_all, bias, slice(rows, 2 * rows))
            stat_out[slot, 0:1, :] = logsum
            stat_out[slot, 1:2, :] = deltas
        for side in range(2):
            stat_link(side, pair).start()

    repeat(0, far_pairs - early, lambda pair: near_queries(pair, lambda at: send_queries(at + early)))
    repeat(far_pairs - early, far_pairs, lambda pair: near_queries(pair, lambda at: None))

    def norm_inner(row, ref, grad, with_gain):
        inverse = inverse_own[row]

        def body(head, total):
            wide, slope = ref[head].astype(jnp.float32), grad[place[head]]
            product = slope * wide
            if with_gain:
                gain_rows[head] = jnp.sum(product * inverse, axis=0, keepdims=True)
            return total + product * gains[row, head]

        total = lax.fori_loop(0, heads, body, jnp.zeros((rows, size), jnp.float32))
        inner = jnp.sum(total, axis=1, keepdims=True) / columns
        shrink[...] = inverse * inverse * inner

    def norm_back(row, ref, grad, out):
        def body(head):
            wide, slope = ref[head].astype(jnp.float32), grad[place[head]]
            result = inverse_own[row] * (slope * gains[row, head] - wide * shrink[...])
            out[:, pl.ds(pl.multiple_of(head * size, size), size)] = result.astype(jnp.bfloat16)

        repeat(0, heads, body)

    norm_inner(0, queries, query_grad, True)

    for owner in range(count):
        tile, offset = divmod(owner * width, LANES)
        part = gain_rows[tile]
        if offset:
            part = pltpu.roll(part, LANES - offset, 1)
        if offset + width > LANES:
            after = pltpu.roll(gain_rows[tile + 1], LANES - offset, 1)
            part = jnp.where(lane < LANES - offset, part, after)
        sum_outbox[owner] = part
    sum_inbox[pl.ds(me, 1)] = sum_outbox[pl.ds(me, 1)]
    repeat(0, count - 1, lambda step: sum_link(step).start())
    norm_back(0, queries, query_grad, d_queries)

    def near_keys(pair):
        for side in range(2):
            link(QUERIES, 1 - side, pair).wait_recv()
            link(UPSTREAM, 1 - side, pair).wait_recv()
            stat_link(1 - side, pair).wait_recv()
        for slot in (2 * pair, 2 * pair + 1):
            head = perm[slot]
            low = normed(query_in[0, slot], inverse_near[0, 0], 0, head)
            high = normed(query_in[1, slot], inverse_near[1, 0], 0, head)
            query_all = jnp.concatenate([low, high], axis=0)
            upstream_all = jnp.concatenate([upstream_in[0, slot], upstream_in[1, slot]], axis=0)
            bias = spatial(slot)
            bias = jnp.concatenate(
                [
                    bias + (frame_bias(slot, 0) - stat_in[0, slot, 0:1, :]),
                    bias + (frame_bias(slot, 2) - stat_in[1, slot, 0:1, :]),
                ],
                axis=1,
            )
            deltas = jnp.concatenate([stat_in[0, slot, 1:2, :], stat_in[1, slot, 1:2, :]], axis=1)
            probs = jnp.exp(dot(key_own[slot], query_all, 1, 1) * factor + bias)
            weights = probs.astype(jnp.bfloat16)
            dprobs = dot(value_own[slot], upstream_all, 1, 1)
            dscores = (probs * (dprobs - deltas)).astype(jnp.bfloat16)
            key_grad[slot] += dot(dscores, query_all, 1, 0) * factor
            value_grad[slot] += dot(weights, upstream_all, 1, 0)

    midway = (2 * far_pairs + 2) // 3
    repeat(0, midway, near_keys)
    repeat(0, count - 1, lambda step: sum_link(step).wait())
    sum_mine[...] = jnp.sum(sum_inbox[...], axis=0)
    repeat(1, group, lambda step: seq_link(step).start())
    sum_inbox_seq[pl.ds(rank, 1)] = sum_mine[...][None]
    repeat(midway, far_pairs, near_keys)
    norm_inner(1, keys, key_grad, False)
    norm_back(1, keys, key_grad, d_keys)

    def finish_values(head):
        out = value_grad[place[head]].astype(jnp.bfloat16)
        d_values[:, pl.ds(pl.multiple_of(head * size, size), size)] = out

    repeat(0, heads, finish_values)

    def sent(pair):
        for side in range(2):
            for which in range(4):
                link(which, side, pair).wait_send()
            stat_link(side, pair).wait_send()

    repeat(0, far_pairs, sent)
    for side in range(2):
        inverse_link(side).wait_send()
    repeat(1, group, lambda step: seq_link(step).wait())
    total = jnp.sum(sum_inbox_seq[...], axis=0)[:, 0:width]
    d_gains[0:1, 0:width] = total
    d_gains[1:2, 0:width] = total * (q_gain[...] / k_gain[...])


def attention(far, identity, perm, place, limits, queries, keys, values, upstream, q_gain, k_gain):
    count, group = lax.axis_size("fsdp"), lax.axis_size("seq")
    heads = limits.shape[0]
    rows, columns = queries.shape
    size = columns // heads
    width = q_gain.shape[0]
    wide, narrow = jnp.float32, jnp.bfloat16
    pairs = far // 2
    smem = pl.BlockSpec(memory_space=pltpu.SMEM)
    hbm = pl.BlockSpec(memory_space=pl.ANY)
    vmem = pl.BlockSpec(memory_space=pltpu.VMEM)
    block = (rows, size)
    dma = pltpu.SemaphoreType.DMA
    scratch = [
        pltpu.VMEM((heads,) + block, narrow),
        pltpu.VMEM((heads,) + block, narrow),
        pltpu.VMEM((heads,) + block, narrow),
        pltpu.VMEM((heads,) + block, narrow),
        pltpu.VMEM((far,) + block, narrow),
        pltpu.VMEM((far,) + block, narrow),
        pltpu.VMEM((heads,) + block, narrow),
        pltpu.VMEM((heads,) + block, narrow),
        pltpu.VMEM((heads,) + block, narrow),
        pltpu.VMEM((heads,) + block, narrow),
        pltpu.VMEM((2, far) + block, narrow),
        pltpu.VMEM((2, far) + block, narrow),
        pltpu.VMEM((2, far) + block, narrow),
        pltpu.VMEM((2, far) + block, narrow),
        pltpu.VMEM((far, 2, size), wide),
        pltpu.VMEM((2, far, 2, size), wide),
        pltpu.VMEM((2, size), wide),
        pltpu.VMEM((2, 2, size), wide),
        pltpu.VMEM((2,) + block, wide),
        pltpu.VMEM((2, 2) + block, wide),
        pltpu.VMEM(block, wide),
        pltpu.VMEM((2, heads, 1, size), wide),
        pltpu.VMEM((heads, 1, size), wide),
        pltpu.VMEM((heads,) + block, wide),
        pltpu.VMEM((heads,) + block, wide),
        pltpu.VMEM((heads,) + block, wide),
        pltpu.VMEM((1, 2 * LANES), wide),
        pltpu.VMEM((count, 1, 2 * LANES), wide),
        pltpu.VMEM((count, 1, LANES), wide),
        pltpu.VMEM((count, 1, LANES), wide),
        pltpu.VMEM((1, LANES), wide),
        pltpu.VMEM((group, 1, LANES), wide),
        dma((4, heads)),
        dma((4, 2, pairs)),
        dma((4, 2, pairs)),
        dma((2, pairs)),
        dma((2, pairs)),
        dma((2,)),
        dma((2,)),
        dma((count,)),
        dma((count,)),
        dma((count,)),
        dma((count,)),
        dma((group,)),
        dma((group,)),
    ]
    return pl.pallas_call(
        functools.partial(attention_kernel, far, count, group),
        out_shape=[jax.ShapeDtypeStruct((rows, columns), narrow)] * 3
        + [jax.ShapeDtypeStruct((2, LANES), wide)],
        in_specs=[smem] * 2 + [vmem] + [hbm] * 4 + [vmem] * 2,
        out_specs=[vmem] * 4,
        scratch_shapes=scratch,
        compiler_params=pltpu.CompilerParams(
            collective_id=identity, has_side_effects=True, vmem_limit_bytes=56 * 1024 * 1024
        ),
        name="attention_backward",
    )(perm, place, limits, queries, keys, values, upstream, q_gain[None], k_gain[None])

def order_kernel(capacities, windows, length, perm, place, branch, limits):
    rank, group = lax.axis_index("seq"), lax.axis_size("seq")
    heads = windows.shape[0]
    near = 0
    for head in range(heads):
        near = near + (windows[head, 0] >= 1).astype(jnp.int32)
    branch[0] = sum((near > at).astype(jnp.int32) for at in capacities[:-1])
    frames = length[0]
    own = rank < frames
    below = (rank > 0) & own
    above = (rank + 1 < group) & (rank + 1 < frames)
    ahead, behind = 0, near
    for head in range(heads):
        reaches = windows[head, 0] >= 1
        slot = jnp.where(reaches, ahead, behind)
        ahead = ahead + reaches.astype(jnp.int32)
        behind = behind + 1 - reaches.astype(jnp.int32)
        perm[slot] = head
        place[head] = slot
        frame_bias = [jnp.where(seen, 0.0, BLOCKED) for seen in (reaches & below, own, reaches & above)]
        widths = [windows[head, 1].astype(jnp.float32), windows[head, 2].astype(jnp.float32)]
        for row, value in enumerate(frame_bias + widths):
            limits[slot, row : row + 1, :] = jnp.full((1, LANES), value, jnp.float32)


def head_order(windows, lengths, capacities):
    heads = windows.shape[0]
    smem = pl.BlockSpec(memory_space=pltpu.SMEM)
    return pl.pallas_call(
        functools.partial(order_kernel, capacities),
        out_shape=[
            jax.ShapeDtypeStruct((heads,), jnp.int32),
            jax.ShapeDtypeStruct((heads,), jnp.int32),
            jax.ShapeDtypeStruct((1,), jnp.int32),
            jax.ShapeDtypeStruct((heads, 8, LANES), jnp.float32),
        ],
        in_specs=[smem] * 2,
        out_specs=[smem] * 3 + [pl.BlockSpec(memory_space=pltpu.VMEM)],
        name="head_order",
    )(windows, lengths)


def deliver_kernel(width, *refs):
    sources, gains, targets, q_gain, k_gain, sems = refs[0:3], refs[3], refs[4:7], refs[7], refs[8], refs[9]
    copies = [pltpu.make_async_copy(sources[at], targets[at], sems.at[at]) for at in range(3)]
    for copy in copies:
        copy.start()
    q_gain[...] = gains[0:1, 0:width]
    k_gain[...] = gains[1:2, 0:width]
    for copy in copies:
        copy.wait()


def deliver(width, *results):
    hbm, vmem = pl.BlockSpec(memory_space=pl.ANY), pl.BlockSpec(memory_space=pltpu.VMEM)
    gain = jax.ShapeDtypeStruct((1, width), jnp.float32)
    return pl.pallas_call(
        functools.partial(deliver_kernel, width),
        out_shape=[jax.ShapeDtypeStruct(result.shape, result.dtype) for result in results[:3]] + [gain] * 2,
        in_specs=[hbm] * 3 + [vmem],
        out_specs=[hbm] * 3 + [vmem] * 2,
        scratch_shapes=[pltpu.SemaphoreType.DMA((3,))],
        name="deliver",
    )(*results)


def local(queries, keys, values, grad_out, q_gain, k_gain, lengths, windows):
    shape = queries.shape
    flat = (shape[1] * shape[2], shape[3])
    arrays = [array.reshape(flat) for array in (queries, keys, values, grad_out)]
    heads = windows.shape[0]
    capacities = [at for at in CAPACITIES if at < heads] + [heads]
    perm, place, branch, limits = head_order(windows, lengths, capacities)
    results = lax.switch(
        branch[0],
        [functools.partial(attention, far, at) for at, far in enumerate(capacities)],
        perm,
        place,
        limits,
        *arrays,
        q_gain,
        k_gain,
    )
    d_queries, d_keys, d_values, d_q_gain, d_k_gain = deliver(q_gain.shape[0], *results)
    return (
        d_queries.reshape(shape),
        d_keys.reshape(shape),
        d_values.reshape(shape),
        d_q_gain[0],
        d_k_gain[0],
    )


def solution(mesh):
    in_specs = (
        P("fsdp", "seq", None, None),
        P("fsdp", "seq", None, None),
        P("fsdp", "seq", None, None),
        P("fsdp", "seq", None, None),
        P("fsdp"),
        P("fsdp"),
        P("fsdp"),
        P(),
    )
    out_specs = (
        P("fsdp", "seq", None, None),
        P("fsdp", "seq", None, None),
        P("fsdp", "seq", None, None),
        P("fsdp"),
        P("fsdp"),
    )
    return jax.shard_map(local, mesh=mesh, in_specs=in_specs, out_specs=out_specs, check_vma=False)
```

```python
import functools

import jax
import jax.numpy as jnp
from jax import lax
from jax.experimental import pallas as pl
from jax.experimental.pallas import tpu as pltpu
from jax.sharding import PartitionSpec as P

PW = 8
TILE_H = 4
TILE_W = 4
LANES = 128
EPS = 1e-06
BLOCKED = -1e30
FLOOR = -1e29
MESH = pl.DeviceIdType.MESH
KEYS, VALUES, QUERIES, UPSTREAM = range(4)
CAPACITIES = (8, 9, 10, 11, 12, 14, 20)


def dot(left, right, left_dim, right_dim):
    return lax.dot_general(
        left, right, (((left_dim,), (right_dim,)), ((), ())), preferred_element_type=jnp.float32
    )


def attention_kernel(
    far,
    count,
    group,
    perm,
    place,
    limits,
    queries_hbm,
    keys_hbm,
    values_hbm,
    upstream_hbm,
    q_gain,
    k_gain,
    d_queries,
    d_keys,
    d_values,
    d_gains,
    keys,
    values,
    queries,
    upstream,
    key_raw,
    query_raw,
    key_own,
    query_own,
    value_own,
    upstream_own,
    key_in,
    value_in,
    query_in,
    upstream_in,
    stat_out,
    stat_in,
    inverse_out,
    inverse_in,
    inverse_own,
    inverse_near,
    shrink,
    spatial_own,
    dprobs_own,
    gains,
    gain_slots,
    gain_rows,
    query_grad,
    key_grad,
    value_grad,
    gain_mine,
    gain_inbox,
    sum_outbox,
    sum_inbox,
    sum_mine,
    sum_inbox_seq,
    load_sem,
    send_sem,
    recv_sem,
    stat_send,
    stat_recv,
    inverse_send,
    inverse_recv,
    gain_send,
    gain_recv,
    sum_send,
    sum_recv,
    seq_send,
    seq_recv,
):
    me = lax.axis_index("fsdp")
    rank = lax.axis_index("seq")
    heads = limits.shape[0]
    rows, columns = queries_hbm.shape
    size = columns // heads
    width = q_gain.shape[1]
    factor = size ** (-0.5)
    far_pairs, odd = far // 2, far % 2
    below, above = lax.rem(rank + group - 1, group), lax.rem(rank + 1, group)
    barrier = pltpu.get_barrier_semaphore()

    def farthest(step):
        return count // 2 + (1 - 2 * (step % 2)) * ((step + 1) // 2)

    def repeat(first, last, body):
        lax.fori_loop(first, last, lambda step, carry: (body(step), carry)[1], 0)

    def repeat_pairs(first, last, body):
        if last > first:
            repeat(first, min(last, far_pairs), body)
        if odd and last > max(first, far_pairs):
            body(far_pairs, 1)

    def by_twos(body):
        repeat(0, heads // 2, lambda step: (body(2 * step), body(2 * step + 1))[0])

    arrays = ((keys_hbm, keys), (values_hbm, values), (queries_hbm, queries), (upstream_hbm, upstream))

    def load(which, head):
        source, target = arrays[which]
        part = pl.ds(pl.multiple_of(head * size, size), size)
        return pltpu.make_async_copy(source.at[:, part], target.at[head], load_sem.at[which, head])

    outgoing = (key_raw, value_own, query_raw, upstream_own)
    incoming = (key_in, value_in, query_in, upstream_in)

    def link(which, side, pair, slots=2):
        part = pl.ds(2 * pair, slots)
        return pltpu.make_async_remote_copy(
            src_ref=outgoing[which].at[part],
            dst_ref=incoming[which].at[1 - side, part],
            send_sem=send_sem.at[which, side, pair],
            recv_sem=recv_sem.at[which, 1 - side, pair],
            device_id={"seq": above if side else below},
            device_id_type=MESH,
        )

    def stat_link(side, pair, slots=2):
        part = pl.ds(2 * pair, slots)
        return pltpu.make_async_remote_copy(
            src_ref=stat_out.at[part],
            dst_ref=stat_in.at[1 - side, part],
            send_sem=stat_send.at[side, pair],
            recv_sem=stat_recv.at[1 - side, pair],
            device_id={"seq": above if side else below},
            device_id_type=MESH,
        )

    def inverse_link(side):
        return pltpu.make_async_remote_copy(
            src_ref=inverse_out,
            dst_ref=inverse_in.at[1 - side],
            send_sem=inverse_send.at[side],
            recv_sem=inverse_recv.at[1 - side],
            device_id={"seq": above if side else below},
            device_id_type=MESH,
        )

    def gain_link(step):
        step = farthest(step)
        return pltpu.make_async_remote_copy(
            src_ref=gain_mine,
            dst_ref=gain_inbox.at[me],
            send_sem=gain_send.at[step],
            recv_sem=gain_recv.at[step],
            device_id={"fsdp": lax.rem(me + step, count)},
            device_id_type=MESH,
        )

    def sum_link(step):
        step = farthest(step)
        peer = lax.rem(me + step, count)
        return pltpu.make_async_remote_copy(
            src_ref=sum_outbox.at[peer],
            dst_ref=sum_inbox.at[me],
            send_sem=sum_send.at[step],
            recv_sem=sum_recv.at[step],
            device_id={"fsdp": peer},
            device_id_type=MESH,
        )

    def seq_link(step):
        return pltpu.make_async_remote_copy(
            src_ref=sum_mine,
            dst_ref=sum_inbox_seq.at[rank],
            send_sem=seq_send.at[step],
            recv_sem=seq_recv.at[step],
            device_id={"seq": lax.rem(rank + step, group)},
            device_id_type=MESH,
        )

    def greet(step):
        peer = lax.rem(me + farthest(step), count)
        pl.semaphore_signal(barrier, inc=1, device_id={"fsdp": peer}, device_id_type=MESH)

    def greet_seq(step):
        peer = lax.rem(rank + step, group)
        pl.semaphore_signal(barrier, inc=1, device_id={"seq": peer}, device_id_type=MESH)

    repeat(0, count - 1, greet)
    repeat(1, group, greet_seq)
    for which in range(4):
        repeat(0, heads, lambda head: load(which, head).start())
    gain_mine[...] = jnp.zeros_like(gain_mine)
    gain_mine[0:1, 0:width] = q_gain[...]
    gain_mine[0:1, LANES : LANES + width] = k_gain[...]
    gain_inbox[pl.ds(me, 1)] = gain_mine[...][None]

    def stage_keys(slot):
        key_raw[slot] = keys[perm[slot]]

    def stage_values(slot):
        value_own[slot] = values[perm[slot]]

    def stage_queries(slot):
        query_raw[slot] = queries[perm[slot]]

    def stage_upstream(slot):
        upstream_own[slot] = upstream[perm[slot]]

    def invert(row, ref):
        def squares(head, total):
            wide = ref[head].astype(jnp.float32)
            return total + wide * wide

        total = lax.fori_loop(0, heads, squares, jnp.zeros((rows, size), jnp.float32))
        mean = jnp.sum(total, axis=1, keepdims=True) / columns
        inverse = jnp.broadcast_to(lax.rsqrt(mean + EPS), (rows, size))
        inverse_own[row] = inverse
        inverse_out[row : row + 1, :] = jnp.transpose(inverse)[0:1, :]

    repeat(0, heads, lambda head: load(KEYS, head).wait())
    repeat(0, far, stage_keys)
    repeat(0, heads, lambda head: load(VALUES, head).wait())
    repeat(0, heads, stage_values)
    invert(1, keys)
    repeat(0, heads, lambda head: load(QUERIES, head).wait())
    invert(0, queries)
    repeat(0, far, stage_queries)
    repeat(0, heads, lambda head: load(UPSTREAM, head).wait())
    repeat(0, heads, stage_upstream)
    pl.semaphore_wait(barrier, count + group - 2)

    def send_keys(pair, slots=2):
        for side in range(2):
            link(KEYS, side, pair, slots).start()
            link(VALUES, side, pair, slots).start()

    def send_queries(pair, slots=2):
        for side in range(2):
            link(QUERIES, side, pair, slots).start()
            link(UPSTREAM, side, pair, slots).start()

    for side in range(2):
        inverse_link(side).start()
    pairs = far_pairs + odd
    repeat_pairs(0, 1, send_keys)
    repeat(0, count - 1, lambda step: gain_link(step).start())
    repeat_pairs(1, pairs, send_keys)

    key_pixel = lax.broadcasted_iota(jnp.int32, (rows, rows), 0)
    query_pixel = lax.broadcasted_iota(jnp.int32, (rows, rows), 1)
    apart_rows = jnp.abs(key_pixel // PW // TILE_H - query_pixel // PW // TILE_H)
    apart_columns = jnp.abs(key_pixel % PW // TILE_W - query_pixel % PW // TILE_W)
    apart_rows = apart_rows.astype(jnp.float32)
    apart_columns = apart_columns.astype(jnp.float32)

    def spatial(head):
        seen = (apart_rows <= limits[head, 3:4, :]) & (apart_columns <= limits[head, 4:5, :])
        return jnp.where(seen, 0.0, BLOCKED)

    def frame_bias(head, frame):
        return limits[head, frame : frame + 1, :]

    def prepare(slot):
        spatial_own[slot] = spatial(slot)
        dprobs_own[slot] = dot(value_own[slot], upstream_own[slot], 1, 1)

    by_twos(prepare)

    repeat(0, count - 1, lambda step: gain_link(step).wait())
    lane = lax.broadcasted_iota(jnp.int32, (1, LANES), 1)
    for row in range(2):
        tiles = [jnp.zeros((1, LANES), jnp.float32) for _ in range(heads + 1)]
        for owner in range(count):
            tile, offset = divmod(owner * width, LANES)
            part = gain_inbox[owner, :, row * LANES : (row + 1) * LANES]
            if offset:
                part = pltpu.roll(part, offset, 1)
            if offset + width > LANES:
                tiles[tile + 1] = tiles[tile + 1] + jnp.where(lane < offset, part, 0.0)
                part = jnp.where(lane >= offset, part, 0.0)
            tiles[tile] = tiles[tile] + part
        for head in range(heads):
            gains[row, head] = tiles[head]

    def normed(raw, inverse, row, head):
        return (raw.astype(jnp.float32) * inverse * gains[row, head]).astype(jnp.bfloat16)

    def normalise(slot):
        head = perm[slot]
        query_own[slot] = normed(queries[head], inverse_own[0], 0, head)
        key_own[slot] = normed(keys[head], inverse_own[1], 1, head)

    by_twos(normalise)

    def soft(scores, bias):
        scores = scores * factor + bias
        top = jnp.maximum(jnp.max(scores, axis=0, keepdims=True), FLOOR)
        raised = jnp.exp(scores - top)
        total = jnp.maximum(jnp.sum(raised, axis=0, keepdims=True), 1e-30)
        return raised * (1.0 / total), top + jnp.log(total)

    def query_side(slot, key_all, dprobs, bias, own):
        query_block, upstream_block = query_own[slot], upstream_own[slot]
        probs, logsum = soft(dot(key_all, query_block, 1, 1), bias)
        weights = probs.astype(jnp.bfloat16)
        deltas = jnp.sum(weights.astype(jnp.float32) * dprobs, axis=0, keepdims=True)
        dscores = (probs * (dprobs - deltas)).astype(jnp.bfloat16)
        query_grad[slot] = dot(dscores, key_all, 0, 0) * factor
        key_grad[slot] = dot(dscores[own], query_block, 1, 0) * factor
        value_grad[slot] = dot(weights[own], upstream_block, 1, 0)
        return logsum, deltas

    def alone(slot):
        bias = spatial_own[slot] + frame_bias(slot, 1)
        query_side(slot, key_own[slot], dprobs_own[slot], bias, slice(0, rows))

    early = pairs // 2
    repeat_pairs(0, early, send_queries)
    if (heads - far) % 2:
        alone(far)
    if heads - far > 1:
        start = heads - (heads - far) // 2 * 2
        repeat(0, (heads - far) // 2, lambda step: (alone(start + 2 * step), alone(start + 2 * step + 1))[0])

    for side in range(2):
        inverse_link(1 - side).wait_recv()
        for row in range(2):
            spread = jnp.broadcast_to(inverse_in[side, row : row + 1, :], (rows, size))
            inverse_near[side, row] = jnp.transpose(spread)

    def near_queries(pair, slots=2):
        for side in range(2):
            link(KEYS, 1 - side, pair, slots).wait_recv()
            link(VALUES, 1 - side, pair, slots).wait_recv()
        for slot in [2 * pair + at for at in range(slots)]:
            head = perm[slot]
            low = normed(key_in[0, slot], inverse_near[0, 1], 1, head)
            high = normed(key_in[1, slot], inverse_near[1, 1], 1, head)
            key_all = jnp.concatenate([low, key_own[slot], high], axis=0)
            dprobs_low = dot(value_in[0, slot], upstream_own[slot], 1, 1)
            dprobs_high = dot(value_in[1, slot], upstream_own[slot], 1, 1)
            dprobs = jnp.concatenate([dprobs_low, dprobs_own[slot], dprobs_high], axis=0)
            bias = spatial_own[slot]
            bias = jnp.concatenate([bias + frame_bias(slot, at) for at in range(3)], axis=0)
            logsum, deltas = query_side(slot, key_all, dprobs, bias, slice(rows, 2 * rows))
            stat_out[slot, 0:1, :] = logsum
            stat_out[slot, 1:2, :] = deltas
        for side in range(2):
            stat_link(side, pair, slots).start()

    def near_queries_sending(pair, slots=2):
        send_queries(pair + early)
        near_queries(pair, slots)

    repeat(0, far_pairs - early, near_queries_sending)
    if odd:
        send_queries(far_pairs, 1)
    repeat_pairs(far_pairs - early, pairs, near_queries)

    def norm_inner(row, ref, grad, with_gain, parts, total):
        inverse = inverse_own[row]

        def body(slot, total):
            head = perm[slot]
            product = ref[head].astype(jnp.float32) * grad[slot]
            if with_gain:
                gain_slots[slot] = jnp.sum(product * inverse, axis=0, keepdims=True)
            return total + product * gains[row, head]

        for first, last in parts:
            total = lax.fori_loop(first, last, body, total)
        return total

    def norm_shrink(row, total):
        inner = jnp.sum(total, axis=1, keepdims=True) / columns
        inverse = inverse_own[row]
        shrink[...] = inverse * inverse * inner

    def norm_back(row, ref, grad, out, beside=None):
        def body(head):
            slot, part = place[head], pl.ds(pl.multiple_of(head * size, size), size)
            wide, slope = ref[head].astype(jnp.float32), grad[slot]
            result = inverse_own[row] * (slope * gains[row, head] - wide * shrink[...])
            out[:, part] = result.astype(jnp.bfloat16)
            if beside is not None:
                beside[1][:, part] = beside[0][slot].astype(jnp.bfloat16)

        by_twos(body)

    nothing = jnp.zeros((rows, size), jnp.float32)
    total = norm_inner(0, queries, query_grad, True, [(0, heads)], nothing)
    repeat(0, heads, lambda head: gain_rows.__setitem__(head, gain_slots[place[head]]))

    for owner in range(count):
        tile, offset = divmod(owner * width, LANES)
        part = gain_rows[tile]
        if offset:
            part = pltpu.roll(part, LANES - offset, 1)
        if offset + width > LANES:
            after = pltpu.roll(gain_rows[tile + 1], LANES - offset, 1)
            part = jnp.where(lane < LANES - offset, part, after)
        sum_outbox[owner] = part
    sum_inbox[pl.ds(me, 1)] = sum_outbox[pl.ds(me, 1)]
    repeat(0, count - 1, lambda step: sum_link(step).start())
    norm_shrink(0, total)
    norm_back(0, queries, query_grad, d_queries)

    def near_keys(pair, slots=2):
        for side in range(2):
            link(QUERIES, 1 - side, pair, slots).wait_recv()
            link(UPSTREAM, 1 - side, pair, slots).wait_recv()
            stat_link(1 - side, pair, slots).wait_recv()
        for slot in [2 * pair + at for at in range(slots)]:
            head = perm[slot]
            low = normed(query_in[0, slot], inverse_near[0, 0], 0, head)
            high = normed(query_in[1, slot], inverse_near[1, 0], 0, head)
            query_all = jnp.concatenate([low, high], axis=0)
            upstream_all = jnp.concatenate([upstream_in[0, slot], upstream_in[1, slot]], axis=0)
            bias = spatial_own[slot]
            bias = jnp.concatenate(
                [
                    bias + (frame_bias(slot, 0) - stat_in[0, slot, 0:1, :]),
                    bias + (frame_bias(slot, 2) - stat_in[1, slot, 0:1, :]),
                ],
                axis=1,
            )
            deltas = jnp.concatenate([stat_in[0, slot, 1:2, :], stat_in[1, slot, 1:2, :]], axis=1)
            probs = jnp.exp(dot(key_own[slot], query_all, 1, 1) * factor + bias)
            weights = probs.astype(jnp.bfloat16)
            dprobs = dot(value_own[slot], upstream_all, 1, 1)
            dscores = (probs * (dprobs - deltas)).astype(jnp.bfloat16)
            key_grad[slot] += dot(dscores, query_all, 1, 0) * factor
            value_grad[slot] += dot(weights, upstream_all, 1, 0)

    repeat_pairs(0, pairs - 1, near_keys)
    last = 2 * (pairs - 1)
    total = norm_inner(1, keys, key_grad, False, [(0, last), (far, heads)], nothing)
    repeat(0, count - 1, lambda step: sum_link(step).wait())
    sum_mine[...] = jnp.sum(sum_inbox[...], axis=0)
    repeat(1, group, lambda step: seq_link(step).start())
    sum_inbox_seq[pl.ds(rank, 1)] = sum_mine[...][None]
    repeat_pairs(pairs - 1, pairs, near_keys)
    norm_shrink(1, norm_inner(1, keys, key_grad, False, [(last, far)], total))
    norm_back(1, keys, key_grad, d_keys, (value_grad, d_values))

    def sent(pair, slots=2):
        for side in range(2):
            for which in range(4):
                link(which, side, pair, slots).wait_send()
            stat_link(side, pair, slots).wait_send()

    repeat_pairs(0, pairs, sent)
    for side in range(2):
        inverse_link(side).wait_send()
    repeat(1, group, lambda step: seq_link(step).wait())
    total = jnp.sum(sum_inbox_seq[...], axis=0)[:, 0:width]
    d_gains[0:1, 0:width] = total
    d_gains[1:2, 0:width] = total * (q_gain[...] / k_gain[...])


def attention(far, identity, perm, place, limits, queries, keys, values, upstream, q_gain, k_gain):
    count, group = lax.axis_size("fsdp"), lax.axis_size("seq")
    heads = limits.shape[0]
    rows, columns = queries.shape
    size = columns // heads
    width = q_gain.shape[0]
    wide, narrow = jnp.float32, jnp.bfloat16
    pairs = (far + 1) // 2
    smem = pl.BlockSpec(memory_space=pltpu.SMEM)
    hbm = pl.BlockSpec(memory_space=pl.ANY)
    vmem = pl.BlockSpec(memory_space=pltpu.VMEM)
    block = (rows, size)
    dma = pltpu.SemaphoreType.DMA
    scratch = [
        pltpu.VMEM((heads,) + block, narrow),
        pltpu.VMEM((heads,) + block, narrow),
        pltpu.VMEM((heads,) + block, narrow),
        pltpu.VMEM((heads,) + block, narrow),
        pltpu.VMEM((far,) + block, narrow),
        pltpu.VMEM((far,) + block, narrow),
        pltpu.VMEM((heads,) + block, narrow),
        pltpu.VMEM((heads,) + block, narrow),
        pltpu.VMEM((heads,) + block, narrow),
        pltpu.VMEM((heads,) + block, narrow),
        pltpu.VMEM((2, far) + block, narrow),
        pltpu.VMEM((2, far) + block, narrow),
        pltpu.VMEM((2, far) + block, narrow),
        pltpu.VMEM((2, far) + block, narrow),
        pltpu.VMEM((far, 2, size), wide),
        pltpu.VMEM((2, far, 2, size), wide),
        pltpu.VMEM((2, size), wide),
        pltpu.VMEM((2, 2, size), wide),
        pltpu.VMEM((2,) + block, wide),
        pltpu.VMEM((2, 2) + block, wide),
        pltpu.VMEM(block, wide),
        pltpu.VMEM((heads,) + block, wide),
        pltpu.VMEM((heads,) + block, wide),
        pltpu.VMEM((2, heads, 1, size), wide),
        pltpu.VMEM((heads, 1, size), wide),
        pltpu.VMEM((heads, 1, size), wide),
        pltpu.VMEM((heads,) + block, wide),
        pltpu.VMEM((heads,) + block, wide),
        pltpu.VMEM((heads,) + block, wide),
        pltpu.VMEM((1, 2 * LANES), wide),
        pltpu.VMEM((count, 1, 2 * LANES), wide),
        pltpu.VMEM((count, 1, LANES), wide),
        pltpu.VMEM((count, 1, LANES), wide),
        pltpu.VMEM((1, LANES), wide),
        pltpu.VMEM((group, 1, LANES), wide),
        dma((4, heads)),
        dma((4, 2, pairs)),
        dma((4, 2, pairs)),
        dma((2, pairs)),
        dma((2, pairs)),
        dma((2,)),
        dma((2,)),
        dma((count,)),
        dma((count,)),
        dma((count,)),
        dma((count,)),
        dma((group,)),
        dma((group,)),
    ]
    return pl.pallas_call(
        functools.partial(attention_kernel, far, count, group),
        out_shape=[jax.ShapeDtypeStruct((rows, columns), narrow)] * 3
        + [jax.ShapeDtypeStruct((2, LANES), wide)],
        in_specs=[smem] * 2 + [vmem] + [hbm] * 4 + [vmem] * 2,
        out_specs=[vmem] * 4,
        scratch_shapes=scratch,
        compiler_params=pltpu.CompilerParams(
            collective_id=identity, has_side_effects=True, vmem_limit_bytes=56 * 1024 * 1024
        ),
        name="attention_backward",
    )(perm, place, limits, queries, keys, values, upstream, q_gain[None], k_gain[None])

def order_kernel(capacities, windows, length, perm, place, branch, limits):
    rank, group = lax.axis_index("seq"), lax.axis_size("seq")
    heads = windows.shape[1]
    near = 0
    for head in range(heads):
        near = near + (windows[0, head] >= 1).astype(jnp.int32)
    branch[0] = sum((near > at).astype(jnp.int32) for at in capacities[:-1])
    frames = length[0]
    own = rank < frames
    below = (rank > 0) & own
    above = (rank + 1 < group) & (rank + 1 < frames)
    ahead, behind = 0, near
    for head in range(heads):
        reaches = windows[0, head] >= 1
        slot = jnp.where(reaches, ahead, behind)
        ahead = ahead + reaches.astype(jnp.int32)
        behind = behind + 1 - reaches.astype(jnp.int32)
        perm[slot] = head
        place[head] = slot
        frame_bias = [jnp.where(seen, 0.0, BLOCKED) for seen in (reaches & below, own, reaches & above)]
        widths = [windows[1, head].astype(jnp.float32), windows[2, head].astype(jnp.float32)]
        for row, value in enumerate(frame_bias + widths):
            limits[slot, row : row + 1, :] = jnp.full((1, LANES), value, jnp.float32)


def head_order(windows, lengths, capacities):
    heads = windows.shape[0]
    smem = pl.BlockSpec(memory_space=pltpu.SMEM)
    return pl.pallas_call(
        functools.partial(order_kernel, capacities),
        out_shape=[
            jax.ShapeDtypeStruct((heads,), jnp.int32),
            jax.ShapeDtypeStruct((heads,), jnp.int32),
            jax.ShapeDtypeStruct((1,), jnp.int32),
            jax.ShapeDtypeStruct((heads, 8, LANES), jnp.float32),
        ],
        in_specs=[smem] * 2,
        out_specs=[smem] * 3 + [pl.BlockSpec(memory_space=pltpu.VMEM)],
        name="head_order",
    )(windows.T, lengths)


def deliver_kernel(width, *refs):
    sources, gains, targets, q_gain, k_gain, sems = refs[0:3], refs[3], refs[4:7], refs[7], refs[8], refs[9]
    copies = [pltpu.make_async_copy(sources[at], targets[at], sems.at[at]) for at in range(3)]
    for copy in copies:
        copy.start()
    q_gain[...] = gains[0:1, 0:width]
    k_gain[...] = gains[1:2, 0:width]
    for copy in copies:
        copy.wait()


def deliver(width, *results):
    hbm, vmem = pl.BlockSpec(memory_space=pl.ANY), pl.BlockSpec(memory_space=pltpu.VMEM)
    gain = jax.ShapeDtypeStruct((1, width), jnp.float32)
    return pl.pallas_call(
        functools.partial(deliver_kernel, width),
        out_shape=[jax.ShapeDtypeStruct(result.shape, result.dtype) for result in results[:3]] + [gain] * 2,
        in_specs=[hbm] * 3 + [vmem],
        out_specs=[hbm] * 3 + [vmem] * 2,
        scratch_shapes=[pltpu.SemaphoreType.DMA((3,))],
        name="deliver",
    )(*results)


def local(queries, keys, values, grad_out, q_gain, k_gain, lengths, windows):
    shape = queries.shape
    flat = (shape[1] * shape[2], shape[3])
    arrays = [array.reshape(flat) for array in (queries, keys, values, grad_out)]
    heads = windows.shape[0]
    capacities = [at for at in CAPACITIES if at < heads] + [heads]
    perm, place, branch, limits = head_order(windows, lengths, capacities)
    results = lax.switch(
        branch[0],
        [functools.partial(attention, far, at) for at, far in enumerate(capacities)],
        perm,
        place,
        limits,
        *arrays,
        q_gain,
        k_gain,
    )
    d_queries, d_keys, d_values, d_q_gain, d_k_gain = deliver(q_gain.shape[0], *results)
    return (
        d_queries.reshape(shape),
        d_keys.reshape(shape),
        d_values.reshape(shape),
        d_q_gain[0],
        d_k_gain[0],
    )


def solution(mesh):
    in_specs = (
        P("fsdp", "seq", None, None),
        P("fsdp", "seq", None, None),
        P("fsdp", "seq", None, None),
        P("fsdp", "seq", None, None),
        P("fsdp"),
        P("fsdp"),
        P("fsdp"),
        P(),
    )
    out_specs = (
        P("fsdp", "seq", None, None),
        P("fsdp", "seq", None, None),
        P("fsdp", "seq", None, None),
        P("fsdp"),
        P("fsdp"),
    )
    return jax.shard_map(local, mesh=mesh, in_specs=in_specs, out_specs=out_specs, check_vma=False)
```

```python
import functools

import jax
import jax.numpy as jnp
from jax import lax
from jax.experimental import pallas as pl
from jax.experimental.pallas import tpu as pltpu
from jax.sharding import PartitionSpec as P

PW = 8
TILE_H = 4
TILE_W = 4
LANES = 128
EPS = 1e-06
BLOCKED = -1e30
FLOOR = -1e29
MESH = pl.DeviceIdType.MESH
KEYS, VALUES, QUERIES, UPSTREAM = range(4)
CAPACITIES = (9, 10, 11, 12, 14, 20)


def dot(left, right, left_dim, right_dim):
    return lax.dot_general(
        left, right, (((left_dim,), (right_dim,)), ((), ())), preferred_element_type=jnp.float32
    )


def attention_kernel(
    far,
    count,
    group,
    perm,
    place,
    limits,
    queries_hbm,
    keys_hbm,
    values_hbm,
    upstream_hbm,
    q_gain,
    k_gain,
    d_queries,
    d_keys,
    d_values,
    d_gains,
    keys,
    values,
    queries,
    upstream,
    key_raw,
    query_raw,
    key_own,
    query_own,
    value_own,
    upstream_own,
    key_in,
    value_in,
    query_in,
    upstream_in,
    stat_out,
    stat_in,
    inverse_out,
    inverse_in,
    inverse_own,
    inverse_near,
    shrink,
    spatial_own,
    dprobs_own,
    gains,
    gain_slots,
    gain_rows,
    query_grad,
    key_grad,
    value_grad,
    gain_mine,
    gain_inbox,
    sum_outbox,
    sum_inbox,
    sum_mine,
    sum_inbox_seq,
    load_sem,
    send_sem,
    recv_sem,
    stat_send,
    stat_recv,
    inverse_send,
    inverse_recv,
    gain_send,
    gain_recv,
    sum_send,
    sum_recv,
    seq_send,
    seq_recv,
):
    me = lax.axis_index("fsdp")
    rank = lax.axis_index("seq")
    heads = limits.shape[0]
    rows, columns = queries_hbm.shape
    size = columns // heads
    width = q_gain.shape[1]
    factor = size ** (-0.5)
    far_pairs, odd = far // 2, far % 2
    below, above = lax.rem(rank + group - 1, group), lax.rem(rank + 1, group)
    barrier = pltpu.get_barrier_semaphore()

    def farthest(step):
        return count // 2 + (1 - 2 * (step % 2)) * ((step + 1) // 2)

    def repeat(first, last, body):
        lax.fori_loop(first, last, lambda step, carry: (body(step), carry)[1], 0)

    def repeat_pairs(first, last, body):
        if last > first:
            repeat(first, min(last, far_pairs), body)
        if odd and last > max(first, far_pairs):
            body(far_pairs, 1)

    def by_twos(body):
        repeat(0, heads // 2, lambda step: (body(2 * step), body(2 * step + 1))[0])

    arrays = ((keys_hbm, keys), (values_hbm, values), (queries_hbm, queries), (upstream_hbm, upstream))

    def load(which, head):
        source, target = arrays[which]
        part = pl.ds(pl.multiple_of(head * size, size), size)
        return pltpu.make_async_copy(source.at[:, part], target.at[head], load_sem.at[which, head])

    outgoing = (key_raw, value_own, query_raw, upstream_own)
    incoming = (key_in, value_in, query_in, upstream_in)

    def link(which, side, pair, slots=2):
        part = pl.ds(2 * pair, slots)
        return pltpu.make_async_remote_copy(
            src_ref=outgoing[which].at[part],
            dst_ref=incoming[which].at[1 - side, part],
            send_sem=send_sem.at[which, side, pair],
            recv_sem=recv_sem.at[which, 1 - side, pair],
            device_id={"seq": above if side else below},
            device_id_type=MESH,
        )

    def stat_link(side, pair, slots=2):
        part = pl.ds(2 * pair, slots)
        return pltpu.make_async_remote_copy(
            src_ref=stat_out.at[part],
            dst_ref=stat_in.at[1 - side, part],
            send_sem=stat_send.at[side, pair],
            recv_sem=stat_recv.at[1 - side, pair],
            device_id={"seq": above if side else below},
            device_id_type=MESH,
        )

    def inverse_link(side):
        return pltpu.make_async_remote_copy(
            src_ref=inverse_out,
            dst_ref=inverse_in.at[1 - side],
            send_sem=inverse_send.at[side],
            recv_sem=inverse_recv.at[1 - side],
            device_id={"seq": above if side else below},
            device_id_type=MESH,
        )

    def gain_link(step):
        step = farthest(step)
        return pltpu.make_async_remote_copy(
            src_ref=gain_mine,
            dst_ref=gain_inbox.at[me],
            send_sem=gain_send.at[step],
            recv_sem=gain_recv.at[step],
            device_id={"fsdp": lax.rem(me + step, count)},
            device_id_type=MESH,
        )

    def sum_link(step):
        step = farthest(step)
        peer = lax.rem(me + step, count)
        return pltpu.make_async_remote_copy(
            src_ref=sum_outbox.at[peer],
            dst_ref=sum_inbox.at[me],
            send_sem=sum_send.at[step],
            recv_sem=sum_recv.at[step],
            device_id={"fsdp": peer},
            device_id_type=MESH,
        )

    def seq_link(step):
        return pltpu.make_async_remote_copy(
            src_ref=sum_mine,
            dst_ref=sum_inbox_seq.at[rank],
            send_sem=seq_send.at[step],
            recv_sem=seq_recv.at[step],
            device_id={"seq": lax.rem(rank + step, group)},
            device_id_type=MESH,
        )

    def greet(step):
        peer = lax.rem(me + farthest(step), count)
        pl.semaphore_signal(barrier, inc=1, device_id={"fsdp": peer}, device_id_type=MESH)

    def greet_seq(step):
        peer = lax.rem(rank + step, group)
        pl.semaphore_signal(barrier, inc=1, device_id={"seq": peer}, device_id_type=MESH)

    repeat(0, count - 1, greet)
    repeat(1, group, greet_seq)
    for which in range(4):
        repeat(0, heads, lambda head: load(which, head).start())
    gain_mine[...] = jnp.zeros_like(gain_mine)
    gain_mine[0:1, 0:width] = q_gain[...]
    gain_mine[0:1, LANES : LANES + width] = k_gain[...]
    gain_inbox[pl.ds(me, 1)] = gain_mine[...][None]

    def stage_keys(slot):
        key_raw[slot] = keys[perm[slot]]

    def stage_values(slot):
        value_own[slot] = values[perm[slot]]

    def stage_queries(slot):
        query_raw[slot] = queries[perm[slot]]

    def stage_upstream(slot):
        upstream_own[slot] = upstream[perm[slot]]

    def invert(row, ref):
        def squares(head, total):
            wide = ref[head].astype(jnp.float32)
            return total + wide * wide

        total = lax.fori_loop(0, heads, squares, jnp.zeros((rows, size), jnp.float32))
        mean = jnp.sum(total, axis=1, keepdims=True) / columns
        inverse = jnp.broadcast_to(lax.rsqrt(mean + EPS), (rows, size))
        inverse_own[row] = inverse
        inverse_out[row : row + 1, :] = jnp.transpose(inverse)[0:1, :]

    repeat(0, heads, lambda head: load(KEYS, head).wait())
    repeat(0, far, stage_keys)
    repeat(0, heads, lambda head: load(VALUES, head).wait())
    repeat(0, heads, stage_values)
    invert(1, keys)
    repeat(0, heads, lambda head: load(QUERIES, head).wait())
    invert(0, queries)
    repeat(0, far, stage_queries)
    repeat(0, heads, lambda head: load(UPSTREAM, head).wait())
    repeat(0, heads, stage_upstream)
    pl.semaphore_wait(barrier, count + group - 2)

    def send_keys(pair, slots=2):
        for side in range(2):
            link(KEYS, side, pair, slots).start()
            link(VALUES, side, pair, slots).start()

    def send_queries(pair, slots=2):
        for side in range(2):
            link(QUERIES, side, pair, slots).start()
            link(UPSTREAM, side, pair, slots).start()

    for side in range(2):
        inverse_link(side).start()
    pairs = far_pairs + odd
    repeat_pairs(0, 1, send_keys)
    repeat(0, count - 1, lambda step: gain_link(step).start())
    repeat_pairs(1, pairs, send_keys)

    key_pixel = lax.broadcasted_iota(jnp.int32, (rows, rows), 0)
    query_pixel = lax.broadcasted_iota(jnp.int32, (rows, rows), 1)
    apart_rows = jnp.abs(key_pixel // PW // TILE_H - query_pixel // PW // TILE_H)
    apart_columns = jnp.abs(key_pixel % PW // TILE_W - query_pixel % PW // TILE_W)
    apart_rows = apart_rows.astype(jnp.float32)
    apart_columns = apart_columns.astype(jnp.float32)

    def spatial(head):
        seen = (apart_rows <= limits[head, 3:4, :]) & (apart_columns <= limits[head, 4:5, :])
        return jnp.where(seen, 0.0, BLOCKED)

    def frame_bias(head, frame):
        return limits[head, frame : frame + 1, :]

    def prepare(slot):
        spatial_own[slot] = spatial(slot)
        dprobs_own[slot] = dot(value_own[slot], upstream_own[slot], 1, 1)

    by_twos(prepare)

    repeat(0, count - 1, lambda step: gain_link(step).wait())
    lane = lax.broadcasted_iota(jnp.int32, (1, LANES), 1)
    for row in range(2):
        tiles = [jnp.zeros((1, LANES), jnp.float32) for _ in range(heads + 1)]
        for owner in range(count):
            tile, offset = divmod(owner * width, LANES)
            part = gain_inbox[owner, :, row * LANES : (row + 1) * LANES]
            if offset:
                part = pltpu.roll(part, offset, 1)
            if offset + width > LANES:
                tiles[tile + 1] = tiles[tile + 1] + jnp.where(lane < offset, part, 0.0)
                part = jnp.where(lane >= offset, part, 0.0)
            tiles[tile] = tiles[tile] + part
        for head in range(heads):
            gains[row, head] = tiles[head]

    def normed(raw, inverse, row, head):
        return (raw.astype(jnp.float32) * inverse * gains[row, head]).astype(jnp.bfloat16)

    def normalise(slot):
        head = perm[slot]
        query_own[slot] = normed(queries[head], inverse_own[0], 0, head)
        key_own[slot] = normed(keys[head], inverse_own[1], 1, head)

    by_twos(normalise)

    def soft(scores, bias):
        scores = scores * factor + bias
        top = jnp.maximum(jnp.max(scores, axis=0, keepdims=True), FLOOR)
        raised = jnp.exp(scores - top)
        total = jnp.maximum(jnp.sum(raised, axis=0, keepdims=True), 1e-30)
        return raised * (1.0 / total), top + jnp.log(total)

    def query_side(slot, key_all, dprobs, bias, own):
        query_block, upstream_block = query_own[slot], upstream_own[slot]
        probs, logsum = soft(dot(key_all, query_block, 1, 1), bias)
        weights = probs.astype(jnp.bfloat16)
        deltas = jnp.sum(weights.astype(jnp.float32) * dprobs, axis=0, keepdims=True)
        dscores = (probs * (dprobs - deltas)).astype(jnp.bfloat16)
        query_grad[slot] = dot(dscores, key_all, 0, 0) * factor
        key_grad[slot] = dot(dscores[own], query_block, 1, 0) * factor
        value_grad[slot] = dot(weights[own], upstream_block, 1, 0)
        return logsum, deltas

    def alone(slot):
        bias = spatial_own[slot] + frame_bias(slot, 1)
        query_side(slot, key_own[slot], dprobs_own[slot], bias, slice(0, rows))

    early = pairs // 2
    repeat_pairs(0, early, send_queries)
    if (heads - far) % 2:
        alone(far)
    if heads - far > 1:
        start = heads - (heads - far) // 2 * 2
        repeat(0, (heads - far) // 2, lambda step: (alone(start + 2 * step), alone(start + 2 * step + 1))[0])

    for side in range(2):
        inverse_link(1 - side).wait_recv()
        for row in range(2):
            spread = jnp.broadcast_to(inverse_in[side, row : row + 1, :], (rows, size))
            inverse_near[side, row] = jnp.transpose(spread)

    def near_queries(pair, slots=2):
        for side in range(2):
            link(KEYS, 1 - side, pair, slots).wait_recv()
            link(VALUES, 1 - side, pair, slots).wait_recv()
        for slot in [2 * pair + at for at in range(slots)]:
            head = perm[slot]
            low = normed(key_in[0, slot], inverse_near[0, 1], 1, head)
            high = normed(key_in[1, slot], inverse_near[1, 1], 1, head)
            key_all = jnp.concatenate([low, key_own[slot], high], axis=0)
            dprobs_low = dot(value_in[0, slot], upstream_own[slot], 1, 1)
            dprobs_high = dot(value_in[1, slot], upstream_own[slot], 1, 1)
            dprobs = jnp.concatenate([dprobs_low, dprobs_own[slot], dprobs_high], axis=0)
            bias = spatial_own[slot]
            bias = jnp.concatenate([bias + frame_bias(slot, at) for at in range(3)], axis=0)
            logsum, deltas = query_side(slot, key_all, dprobs, bias, slice(rows, 2 * rows))
            stat_out[slot, 0:1, :] = logsum
            stat_out[slot, 1:2, :] = deltas
        for side in range(2):
            stat_link(side, pair, slots).start()

    def near_queries_sending(pair, slots=2):
        send_queries(pair + early)
        near_queries(pair, slots)

    repeat(0, far_pairs - early, near_queries_sending)
    if odd:
        send_queries(far_pairs, 1)
    repeat_pairs(far_pairs - early, pairs, near_queries)

    def norm_inner(row, ref, grad, with_gain, parts, total):
        inverse = inverse_own[row]

        def body(slot, total):
            head = perm[slot]
            product = ref[head].astype(jnp.float32) * grad[slot]
            if with_gain:
                gain_slots[slot] = jnp.sum(product * inverse, axis=0, keepdims=True)
            return total + product * gains[row, head]

        for first, last in parts:
            total = lax.fori_loop(first, last, body, total)
        return total

    def norm_shrink(row, total):
        inner = jnp.sum(total, axis=1, keepdims=True) / columns
        inverse = inverse_own[row]
        shrink[...] = inverse * inverse * inner

    def norm_back(row, ref, grad, out, beside=None):
        def body(head):
            slot, part = place[head], pl.ds(pl.multiple_of(head * size, size), size)
            wide, slope = ref[head].astype(jnp.float32), grad[slot]
            result = inverse_own[row] * (slope * gains[row, head] - wide * shrink[...])
            out[:, part] = result.astype(jnp.bfloat16)
            if beside is not None:
                beside[1][:, part] = beside[0][slot].astype(jnp.bfloat16)

        by_twos(body)

    nothing = jnp.zeros((rows, size), jnp.float32)
    total = norm_inner(0, queries, query_grad, True, [(0, heads)], nothing)
    repeat(0, heads, lambda head: gain_rows.__setitem__(head, gain_slots[place[head]]))

    for owner in range(count):
        tile, offset = divmod(owner * width, LANES)
        part = gain_rows[tile]
        if offset:
            part = pltpu.roll(part, LANES - offset, 1)
        if offset + width > LANES:
            after = pltpu.roll(gain_rows[tile + 1], LANES - offset, 1)
            part = jnp.where(lane < LANES - offset, part, after)
        sum_outbox[owner] = part
    sum_inbox[pl.ds(me, 1)] = sum_outbox[pl.ds(me, 1)]
    repeat(0, count - 1, lambda step: sum_link(step).start())
    norm_shrink(0, total)
    norm_back(0, queries, query_grad, d_queries)

    def near_keys(pair, slots=2):
        for side in range(2):
            link(QUERIES, 1 - side, pair, slots).wait_recv()
            link(UPSTREAM, 1 - side, pair, slots).wait_recv()
            stat_link(1 - side, pair, slots).wait_recv()
        for slot in [2 * pair + at for at in range(slots)]:
            head = perm[slot]
            low = normed(query_in[0, slot], inverse_near[0, 0], 0, head)
            high = normed(query_in[1, slot], inverse_near[1, 0], 0, head)
            query_all = jnp.concatenate([low, high], axis=0)
            upstream_all = jnp.concatenate([upstream_in[0, slot], upstream_in[1, slot]], axis=0)
            bias = spatial_own[slot]
            bias = jnp.concatenate(
                [
                    bias + (frame_bias(slot, 0) - stat_in[0, slot, 0:1, :]),
                    bias + (frame_bias(slot, 2) - stat_in[1, slot, 0:1, :]),
                ],
                axis=1,
            )
            deltas = jnp.concatenate([stat_in[0, slot, 1:2, :], stat_in[1, slot, 1:2, :]], axis=1)
            probs = jnp.exp(dot(key_own[slot], query_all, 1, 1) * factor + bias)
            weights = probs.astype(jnp.bfloat16)
            dprobs = dot(value_own[slot], upstream_all, 1, 1)
            dscores = (probs * (dprobs - deltas)).astype(jnp.bfloat16)
            key_grad[slot] += dot(dscores, query_all, 1, 0) * factor
            value_grad[slot] += dot(weights, upstream_all, 1, 0)

    def sent(pair, slots=2):
        for side in range(2):
            for which in range(4):
                link(which, side, pair, slots).wait_send()
            stat_link(side, pair, slots).wait_send()

    repeat_pairs(0, pairs - 1, near_keys)
    last = 2 * (pairs - 1)
    total = norm_inner(1, keys, key_grad, False, [(0, last), (far, heads)], nothing)
    repeat(0, count - 1, lambda step: sum_link(step).wait())
    sum_mine[...] = jnp.sum(sum_inbox[...], axis=0)
    repeat(1, group, lambda step: seq_link(step).start())
    sum_inbox_seq[pl.ds(rank, 1)] = sum_mine[...][None]
    repeat_pairs(0, pairs - 1, sent)
    repeat_pairs(pairs - 1, pairs, near_keys)
    norm_shrink(1, norm_inner(1, keys, key_grad, False, [(last, far)], total))
    norm_back(1, keys, key_grad, d_keys, (value_grad, d_values))

    repeat_pairs(pairs - 1, pairs, sent)
    for side in range(2):
        inverse_link(side).wait_send()
    repeat(1, group, lambda step: seq_link(step).wait())
    total = jnp.sum(sum_inbox_seq[...], axis=0)[:, 0:width]
    d_gains[0:1, 0:width] = total
    d_gains[1:2, 0:width] = total * (q_gain[...] / k_gain[...])


def attention(far, identity, perm, place, limits, queries, keys, values, upstream, q_gain, k_gain):
    count, group = lax.axis_size("fsdp"), lax.axis_size("seq")
    heads = limits.shape[0]
    rows, columns = queries.shape
    size = columns // heads
    width = q_gain.shape[0]
    wide, narrow = jnp.float32, jnp.bfloat16
    pairs = (far + 1) // 2
    smem = pl.BlockSpec(memory_space=pltpu.SMEM)
    hbm = pl.BlockSpec(memory_space=pl.ANY)
    vmem = pl.BlockSpec(memory_space=pltpu.VMEM)
    block = (rows, size)
    dma = pltpu.SemaphoreType.DMA
    scratch = [
        pltpu.VMEM((heads,) + block, narrow),
        pltpu.VMEM((heads,) + block, narrow),
        pltpu.VMEM((heads,) + block, narrow),
        pltpu.VMEM((heads,) + block, narrow),
        pltpu.VMEM((far,) + block, narrow),
        pltpu.VMEM((far,) + block, narrow),
        pltpu.VMEM((heads,) + block, narrow),
        pltpu.VMEM((heads,) + block, narrow),
        pltpu.VMEM((heads,) + block, narrow),
        pltpu.VMEM((heads,) + block, narrow),
        pltpu.VMEM((2, far) + block, narrow),
        pltpu.VMEM((2, far) + block, narrow),
        pltpu.VMEM((2, far) + block, narrow),
        pltpu.VMEM((2, far) + block, narrow),
        pltpu.VMEM((far, 2, size), wide),
        pltpu.VMEM((2, far, 2, size), wide),
        pltpu.VMEM((2, size), wide),
        pltpu.VMEM((2, 2, size), wide),
        pltpu.VMEM((2,) + block, wide),
        pltpu.VMEM((2, 2) + block, wide),
        pltpu.VMEM(block, wide),
        pltpu.VMEM((heads,) + block, wide),
        pltpu.VMEM((heads,) + block, wide),
        pltpu.VMEM((2, heads, 1, size), wide),
        pltpu.VMEM((heads, 1, size), wide),
        pltpu.VMEM((heads, 1, size), wide),
        pltpu.VMEM((heads,) + block, wide),
        pltpu.VMEM((heads,) + block, wide),
        pltpu.VMEM((heads,) + block, wide),
        pltpu.VMEM((1, 2 * LANES), wide),
        pltpu.VMEM((count, 1, 2 * LANES), wide),
        pltpu.VMEM((count, 1, LANES), wide),
        pltpu.VMEM((count, 1, LANES), wide),
        pltpu.VMEM((1, LANES), wide),
        pltpu.VMEM((group, 1, LANES), wide),
        dma((4, heads)),
        dma((4, 2, pairs)),
        dma((4, 2, pairs)),
        dma((2, pairs)),
        dma((2, pairs)),
        dma((2,)),
        dma((2,)),
        dma((count,)),
        dma((count,)),
        dma((count,)),
        dma((count,)),
        dma((group,)),
        dma((group,)),
    ]
    return pl.pallas_call(
        functools.partial(attention_kernel, far, count, group),
        out_shape=[jax.ShapeDtypeStruct((rows, columns), narrow)] * 3
        + [jax.ShapeDtypeStruct((2, LANES), wide)],
        in_specs=[smem] * 2 + [vmem] + [hbm] * 4 + [vmem] * 2,
        out_specs=[vmem] * 4,
        scratch_shapes=scratch,
        compiler_params=pltpu.CompilerParams(
            collective_id=identity, has_side_effects=True, vmem_limit_bytes=56 * 1024 * 1024
        ),
        name="attention_backward",
    )(perm, place, limits, queries, keys, values, upstream, q_gain[None], k_gain[None])

def order_kernel(capacities, windows, length, perm, place, branch, limits):
    rank, group = lax.axis_index("seq"), lax.axis_size("seq")
    heads = windows.shape[1]
    near = 0
    for head in range(heads):
        near = near + (windows[0, head] >= 1).astype(jnp.int32)
    branch[0] = sum((near > at).astype(jnp.int32) for at in capacities[:-1])
    frames = length[0]
    own = rank < frames
    below = (rank > 0) & own
    above = (rank + 1 < group) & (rank + 1 < frames)
    ahead, behind = 0, near
    for head in range(heads):
        reaches = windows[0, head] >= 1
        slot = jnp.where(reaches, ahead, behind)
        ahead = ahead + reaches.astype(jnp.int32)
        behind = behind + 1 - reaches.astype(jnp.int32)
        perm[slot] = head
        place[head] = slot
        frame_bias = [jnp.where(seen, 0.0, BLOCKED) for seen in (reaches & below, own, reaches & above)]
        widths = [windows[1, head].astype(jnp.float32), windows[2, head].astype(jnp.float32)]
        for row, value in enumerate(frame_bias + widths):
            limits[slot, row : row + 1, :] = jnp.full((1, LANES), value, jnp.float32)


def head_order(windows, lengths, capacities):
    heads = windows.shape[0]
    smem = pl.BlockSpec(memory_space=pltpu.SMEM)
    return pl.pallas_call(
        functools.partial(order_kernel, capacities),
        out_shape=[
            jax.ShapeDtypeStruct((heads,), jnp.int32),
            jax.ShapeDtypeStruct((heads,), jnp.int32),
            jax.ShapeDtypeStruct((1,), jnp.int32),
            jax.ShapeDtypeStruct((heads, 8, LANES), jnp.float32),
        ],
        in_specs=[smem] * 2,
        out_specs=[smem] * 3 + [pl.BlockSpec(memory_space=pltpu.VMEM)],
        name="head_order",
    )(windows.T, lengths)


def deliver_kernel(width, *refs):
    sources, gains, targets, q_gain, k_gain, sems = refs[0:3], refs[3], refs[4:7], refs[7], refs[8], refs[9]
    copies = [pltpu.make_async_copy(sources[at], targets[at], sems.at[at]) for at in range(3)]
    for copy in copies:
        copy.start()
    q_gain[...] = gains[0:1, 0:width]
    k_gain[...] = gains[1:2, 0:width]
    for copy in copies:
        copy.wait()


def deliver(width, *results):
    hbm, vmem = pl.BlockSpec(memory_space=pl.ANY), pl.BlockSpec(memory_space=pltpu.VMEM)
    gain = jax.ShapeDtypeStruct((1, width), jnp.float32)
    return pl.pallas_call(
        functools.partial(deliver_kernel, width),
        out_shape=[jax.ShapeDtypeStruct(result.shape, result.dtype) for result in results[:3]] + [gain] * 2,
        in_specs=[hbm] * 3 + [vmem],
        out_specs=[hbm] * 3 + [vmem] * 2,
        scratch_shapes=[pltpu.SemaphoreType.DMA((3,))],
        name="deliver",
    )(*results)


def local(queries, keys, values, grad_out, q_gain, k_gain, lengths, windows):
    shape = queries.shape
    flat = (shape[1] * shape[2], shape[3])
    arrays = [array.reshape(flat) for array in (queries, keys, values, grad_out)]
    heads = windows.shape[0]
    capacities = [at for at in CAPACITIES if at < heads] + [heads]
    perm, place, branch, limits = head_order(windows, lengths, capacities)
    results = lax.switch(
        branch[0],
        [functools.partial(attention, far, at) for at, far in enumerate(capacities)],
        perm,
        place,
        limits,
        *arrays,
        q_gain,
        k_gain,
    )
    d_queries, d_keys, d_values, d_q_gain, d_k_gain = deliver(q_gain.shape[0], *results)
    return (
        d_queries.reshape(shape),
        d_keys.reshape(shape),
        d_values.reshape(shape),
        d_q_gain[0],
        d_k_gain[0],
    )


def solution(mesh):
    in_specs = (
        P("fsdp", "seq", None, None),
        P("fsdp", "seq", None, None),
        P("fsdp", "seq", None, None),
        P("fsdp", "seq", None, None),
        P("fsdp"),
        P("fsdp"),
        P("fsdp"),
        P(),
    )
    out_specs = (
        P("fsdp", "seq", None, None),
        P("fsdp", "seq", None, None),
        P("fsdp", "seq", None, None),
        P("fsdp"),
        P("fsdp"),
    )
    return jax.shard_map(local, mesh=mesh, in_specs=in_specs, out_specs=out_specs, check_vma=False)
```
